256 devices in a mesh: tm: 8 (over x, core), space: 32 (over z, y).
Axes of the slice: x: 4, y: 4, z: 8, core: 2. Of those that a mesh axis runs over, the one named last changes fastest.
Arguments:
- fraction_levels: int32 [8, 128, 16, 1024], P('tm', 'space'), may hold values from 0 to 1024
- start_velocity: float32 [8, 3, 128, 16, 1024], P('tm', None, 'space'), may hold values from -1.8 to 1.8
- electrode_plan: int32 [16, 4, 32], P('tm'), may hold values 0 or 1
Outputs:
- end_fraction: float32 [8, 128, 16, 1024], P('tm', 'space')
- end_velocity: float32 [8, 3, 128, 16, 1024], P('tm', None, 'space')
The draws below stay inside these ranges and needn't reach their ends.
All inputs are finite; a program needn't handle non-finite values. No bound on the sum of `electrode_plan` on one device may be relied on, other than what follows from the above.
Results may differ from the reference program's by a relative error of at most 0.00002.
Values sent between devices are 32-bit elements; how exact they have to be, the bound alone decides.
A program may use at most 128 MiB of HBM per device.

```python
import jax
import jax.numpy as jnp
from jax import lax

NZ = 16
NY = 1024
TILE = 32
FINE = 2
SWEEPS = 4
COARSE_STEPS = 2
NX = 128
SLICES = 8
TX = 4
TY = 32


def touch_ends(drawn, key, low, high):
    extent = drawn.shape
    index_at = [jax.random.randint(jax.random.fold_in(key, axis), (), 0, extent[axis]) for axis in range(len(extent))]
    drawn = drawn.at[tuple(index_at)].set(low)
    longest = extent.index(max(extent))
    index_at[longest] = (index_at[longest] + 1) % extent[longest]
    return drawn.at[tuple(index_at)].set(high)


def steps_of(rng, extent, split, least, high):
    gain, own = 1.0, jax.random.fold_in(rng, 6)
    for dim, shards_of in split:
        steps = jnp.exp(jax.random.uniform(jax.random.fold_in(own, dim), (shards_of,), jnp.float32, least / len(split), high / len(split)))
        gain = gain * jnp.repeat(steps, extent[dim] // shards_of).reshape([-1 if axis == dim else 1 for axis in range(len(extent))])
    return gain


def gaussian(key, shape, spread, reach, pieces=(), kind=jnp.bfloat16):
    loudness = steps_of(key, shape, pieces, -0.22, 0.18) if pieces else 1.0
    entries = jax.random.normal(key, shape, jnp.float32) * spread * loudness
    return jnp.minimum(jnp.maximum(entries, -reach), reach).astype(kind)


def setup_inputs(seed: int = 0) -> dict:
    keys = jax.random.split(jax.random.key(seed), 4)
    return {
        "fraction_levels": touch_ends(jax.random.randint(keys[0], (SLICES, NX, NZ, NY), 0, 1025), jax.random.fold_in(keys[0], 1), 0, 1024).astype(jnp.int32),
        "start_velocity": gaussian(keys[1], (SLICES, 3, NX, NZ, NY), 0.3, 1.8, ((0, 8), (2, 32)), jnp.float32),
        "electrode_plan": touch_ends((jax.random.randint(keys[2], (SLICES * FINE, TX, TY), 0, 2) < 1).astype(jnp.int32), jax.random.fold_in(keys[2], 1), 0, 1),
    }


liquid_density = 1.0
vapour_density = 0.1
viscosity = 0.1
time_step = 0.25
pull_strength = 1.5
wall_decay = 4.0
fraction_spread = 0.05
velocity_spread = 0.15
level_count = 1024.0


def all_pad(array):
    widths = [(0, 0)] * (array.ndim - 3) + [(1, 1), (1, 1), (1, 1)]
    return jnp.pad(array, widths)


def neighbours(padded):
    return (padded[..., 2:, 1:-1, 1:-1] + padded[..., :-2, 1:-1, 1:-1]
            + padded[..., 1:-1, 2:, 1:-1] + padded[..., 1:-1, :-2, 1:-1]
            + padded[..., 1:-1, 1:-1, 2:] + padded[..., 1:-1, 1:-1, :-2])


def centred(padded):
    return jnp.stack([
        0.5 * (padded[2:, 1:-1, 1:-1] - padded[:-2, 1:-1, 1:-1]),
        0.5 * (padded[1:-1, 2:, 1:-1] - padded[1:-1, :-2, 1:-1]),
        0.5 * (padded[1:-1, 1:-1, 2:] - padded[1:-1, 1:-1, :-2])])


def divergence(padded):
    return 0.5 * (padded[0, 2:, 1:-1, 1:-1] - padded[0, :-2, 1:-1, 1:-1]
                  + padded[1, 1:-1, 2:, 1:-1] - padded[1, 1:-1, :-2, 1:-1]
                  + padded[2, 1:-1, 1:-1, 2:] - padded[2, 1:-1, 1:-1, :-2])


def density(fraction):
    return vapour_density + (liquid_density - vapour_density) * jnp.clip(fraction, 0.0, 1.0)


def face_flux(lower, upper, speed_lower, speed_upper):
    speed = 0.5 * (speed_lower + speed_upper)
    return jnp.maximum(speed, 0.0) * lower + jnp.minimum(speed, 0.0) * upper


def advect(cpad, upad):
    flux_x = face_flux(cpad[:-1, 1:-1, 1:-1], cpad[1:, 1:-1, 1:-1], upad[0, :-1, 1:-1, 1:-1], upad[0, 1:, 1:-1, 1:-1])
    flux_z = face_flux(cpad[1:-1, :-1, 1:-1], cpad[1:-1, 1:, 1:-1], upad[1, 1:-1, :-1, 1:-1], upad[1, 1:-1, 1:, 1:-1])
    flux_y = face_flux(cpad[1:-1, 1:-1, :-1], cpad[1:-1, 1:-1, 1:], upad[2, 1:-1, 1:-1, :-1], upad[2, 1:-1, 1:-1, 1:])
    net = (flux_x[1:] - flux_x[:-1] + flux_z[:, 1:] - flux_z[:, :-1]
           + flux_y[:, :, 1:] - flux_y[:, :, :-1])
    return cpad[1:-1, 1:-1, 1:-1] - time_step * net


def momentum(cpad, upad, electrode, wall):
    inner = upad[:, 1:-1, 1:-1, 1:-1]
    laplace = neighbours(upad) - 6.0 * inner
    pull = pull_strength * electrode[:, None, :] * wall[None, :, None] / density(cpad[1:-1, 1:-1, 1:-1])
    return inner + time_step * (viscosity * laplace + pull * centred(cpad))


def coefficients(fpad):
    rho = density(fpad)
    face_x = 2.0 / (rho[:-1, 1:-1, 1:-1] + rho[1:, 1:-1, 1:-1])
    face_z = 2.0 / (rho[1:-1, :-1, 1:-1] + rho[1:-1, 1:, 1:-1])
    face_y = 2.0 / (rho[1:-1, 1:-1, :-1] + rho[1:-1, 1:-1, 1:])
    total = (face_x[:-1] + face_x[1:] + face_z[:, :-1] + face_z[:, 1:]
             + face_y[:, :, :-1] + face_y[:, :, 1:])
    return face_x, face_z, face_y, total


def jacobi(ppad, faces, total, source):
    face_x, face_z, face_y = faces
    summed = (face_x[:-1] * ppad[:-2, 1:-1, 1:-1] + face_x[1:] * ppad[2:, 1:-1, 1:-1]
              + face_z[:, :-1] * ppad[1:-1, :-2, 1:-1] + face_z[:, 1:] * ppad[1:-1, 2:, 1:-1]
              + face_y[:, :, :-1] * ppad[1:-1, 1:-1, :-2] + face_y[:, :, 1:] * ppad[1:-1, 1:-1, 2:])
    return (summed - source) / total


def fine_step(fraction, velocity, electrode, wall):
    padded = all_pad(jnp.concatenate([fraction[None], velocity]))
    new_fraction = advect(padded[0], padded[1:])
    provisional = momentum(padded[0], padded[1:], electrode, wall)
    second = all_pad(jnp.concatenate([new_fraction[None], provisional]))
    face_x, face_z, face_y, total = coefficients(second[0])
    source = divergence(second[1:]) / time_step

    def sweep_once(index, current):
        return jacobi(all_pad(current), (face_x, face_z, face_y), total, source)

    pressure = lax.fori_loop(0, SWEEPS, sweep_once, jnp.zeros_like(new_fraction))
    gradient = centred(all_pad(pressure))
    return new_fraction, provisional - time_step * gradient / density(new_fraction)


def restrict(field):
    parts, rows, layers, columns = field.shape
    blocks = field.reshape(parts, rows // 4, 4, layers // 4, 4, columns // 4, 4)
    return jnp.mean(blocks, axis=(2, 4, 6))


def prolong(coarse):
    parts, rows, layers, columns = coarse.shape
    wide = jnp.broadcast_to(coarse[:, :, None, :, None, :, None], (parts, rows, 4, layers, 4, columns, 4))
    return wide.reshape(parts, rows * 4, layers * 4, columns * 4)


def propagate(coarse):
    spreads = jnp.array([fraction_spread, velocity_spread, velocity_spread, velocity_spread], dtype=jnp.float32)
    spreads = spreads.astype(coarse.dtype)[:, None, None, None]
    for step in range(COARSE_STEPS):
        padded = all_pad(coarse)
        coarse = coarse + spreads * (neighbours(padded) - 6.0 * coarse)
    return coarse


def tile_field(plan_row):
    wide = jnp.repeat(jnp.repeat(plan_row, TILE, axis=0), TILE, axis=1)
    return wide.astype(jnp.float32)


def reference(fraction_levels, start_velocity, electrode_plan):
    wall = jnp.exp(-jnp.arange(NZ, dtype=jnp.float32) / wall_decay)
    plans = electrode_plan.reshape(SLICES, FINE, TX, TY)

    def one_slice(inputs):
        levels, velocity, plan = inputs
        fraction = levels.astype(jnp.float32) / level_count
        start = jnp.concatenate([fraction[None], velocity])
        for step in range(FINE):
            fraction, velocity = fine_step(fraction, velocity, tile_field(plan[step]).astype(velocity.dtype), wall.astype(velocity.dtype))
        finish = jnp.concatenate([fraction[None], velocity])
        return finish, restrict(finish), propagate(restrict(start))

    ends, coarse_ends, coarse_starts = lax.map(one_slice, (fraction_levels, start_velocity, plans))
    later = (jnp.arange(SLICES) > 0).astype(coarse_starts.dtype)[:, None, None, None, None]
    previous = coarse_starts * later
    drive = coarse_ends - previous
    carry = jnp.zeros_like(drive[0])
    results = []
    for index in range(SLICES):
        correction = propagate(carry) - previous[index]
        results.append(ends[index] + prolong(correction))
        carry = propagate(carry) + drive[index]
    corrected = jnp.stack(results)
    return corrected[:, 0], corrected[:, 1:]
```

```python
import functools

import jax
import jax.numpy as jnp
from jax import lax
from jax.experimental import pallas as pl
from jax.experimental.pallas import tpu as pltpu
from jax.sharding import PartitionSpec as P

MESH = pl.DeviceIdType.MESH
F32 = jnp.float32

ROWS = 4
NZ = 16
SUB, LANE = 8, 128
H = 4
EXT = ROWS + 2 * H
TILE = 32
TILES = 4
STRIPS = 32
FINE = 2
U = 4
BLOCKS = NZ // U

SLICES, SPACE = 8, 32
wall_scale = 1.5 * 0.25 * 0.5
wall_decay = 4.0
level_scale = 1.0 / 1024.0
fraction_spread, velocity_spread = 0.05, 0.15


def lane_ids():
    sub = lax.broadcasted_iota(jnp.int32, (SUB, LANE), 0)
    lane = lax.broadcasted_iota(jnp.int32, (SUB, LANE), 1)
    return sub, lane


def roll(v, by, axis):
    return pltpu.roll(v, by, axis)


def next_y(v, masks, fill=0.0, by=1):
    ax = v.ndim
    r = roll(v, LANE - by, ax - 1)
    q = roll(r, SUB - 1, ax - 2)
    q = jnp.where(masks["last_sub"], fill, q)
    return jnp.where(masks["last_lane"] if by == 1 else masks["last_group"], q, r)


def prev_y(v, masks, fill=0.0, by=1):
    ax = v.ndim
    r = roll(v, by, ax - 1)
    q = roll(r, 1, ax - 2)
    q = jnp.where(masks["first_sub"], fill, q)
    return jnp.where(masks["first_lane"] if by == 1 else masks["first_group"], q, r)


def upwind(lower, upper, speed_lower, speed_upper):
    speed = speed_lower + speed_upper
    return speed * jnp.where(speed > 0.0, lower, upper)


def rho_of(c):
    return 0.1 + 0.9 * jnp.clip(c, 0.0, 1.0)


def kernel(
    lev_ref, vel_ref, plan_ref, ofrac_ref, ovel_ref,
    levb, c_a, c_b, u, pv, gx, gz, gyl, gyu, rt, p1, p_a, p_b, elec, wall,
    cstart, prev, drive, rx1, rx2, rxs, rxq, t1, t2, w0, w1,
    in_sem, out_sem, fs_send, fs_recv, cs_send, cs_recv,
):
    t = lax.axis_index("tm")
    s = lax.axis_index("space")
    sub, lane = lane_ids()
    masks = {
        "last_sub": sub == SUB - 1, "first_sub": sub == 0,
        "last_lane": lane == LANE - 1, "first_lane": lane == 0,
        "last_group": lane >= LANE - 4, "first_group": lane < 4,
    }

    def there(dt, ds):
        return (t + dt >= 0) & (t + dt < SLICES) & (s + ds >= 0) & (s + ds < SPACE)

    has_left, has_right = s > 0, s < SPACE - 1

    loads = []
    for k in range(SUB):
        cols = pl.ds(LANE * k, LANE)
        loads.append(pltpu.make_async_copy(lev_ref.at[0, :, :, cols], levb.at[:, :, k, :], in_sem.at[0, k]))
        for d in range(3):
            loads.append(pltpu.make_async_copy(
                vel_ref.at[0, d, :, :, cols], u.at[d, pl.ds(H, ROWS), pl.ds(1, NZ), k, :], in_sem.at[1 + d, k]))
    for c in loads:
        c.start()

    zero_line = jnp.zeros((SUB, LANE), F32)

    def zero_pads(e, _):
        for ref in (c_a, c_b, p1, p_a, p_b, pv.at[1], u.at[0], u.at[1], u.at[2]):
            ref[e, 0] = zero_line
            ref[e, NZ + 1] = zero_line
        return 0

    lax.fori_loop(0, EXT, zero_pads, 0)

    def zero_rows(first):
        def one(j, _):
            z = 1 + lax.rem(j, NZ)
            e = first + lax.div(j, NZ)
            for ref in (c_a, c_b, p1, u.at[0], u.at[1], u.at[2]):
                ref[e, z] = zero_line
            return 0
        lax.fori_loop(0, H * NZ, one, 0)

    @pl.when(s == 0)
    def _():
        zero_rows(0)

    @pl.when(s == SPACE - 1)
    def _():
        zero_rows(H + ROWS)

    zero_coarse = jnp.zeros((4, SUB, LANE), F32)
    for ref in (cstart, rx1, rx2, rxs, rxq):
        def one_row(j, _, ref=ref):
            ref[j] = zero_coarse
            return 0
        lax.fori_loop(0, ref.shape[0], one_row, 0)

    barrier = pltpu.get_barrier_semaphore()
    groups = [(0, 2)] + [(sign * k, r) for k, r in ((1, 2), (2, 4), (4, 8)) for sign in (1, -1)]
    expected = jnp.int32(0)
    for dt, reach in groups:
        def greet(j, count, dt=dt, reach=reach):
            ds = j - reach
            ok = there(dt, ds)
            if dt == 0:
                ok = ok & (ds != 0)

            @pl.when(ok)
            def _():
                pl.semaphore_signal(barrier, inc=1, device_id=(t + dt, s + ds), device_id_type=MESH)

            return count + ok.astype(jnp.int32)
        expected = lax.fori_loop(0, 2 * reach + 1, greet, expected)

    strip = sub * 4 + lax.div(lane, TILE)
    first_row = s * ROWS
    tiles = [jnp.clip(lax.div(first_row - 1 + TILE, TILE) - 1, 0, TILES - 1), lax.div(first_row, TILE),
             jnp.clip(lax.div(first_row + ROWS, TILE), 0, TILES - 1)]
    for f in range(FINE):
        for j, tile in enumerate(tiles):
            def paint(q, field, f=f, tile=tile):
                return jnp.where(strip == q, plan_ref[f, tile, q].astype(F32), field)
            elec[f, j] = lax.fori_loop(0, STRIPS, paint, zero_line)
    for z in range(NZ):
        wall[z] = jnp.full((SUB, LANE), wall_scale, F32) * jnp.exp(jnp.full((SUB, LANE), -z / wall_decay, F32))

    for k in range(SUB):
        loads[4 * k].wait()

    def to_fraction(j, _):
        i, z = lax.div(j, NZ), lax.rem(j, NZ)
        c_a[H + i, 1 + z] = levb[i, z].astype(F32) * level_scale
        return 0

    lax.fori_loop(0, ROWS * NZ, to_fraction, 0)
    for k in range(SUB):
        for d in range(3):
            loads[4 * k + 1 + d].wait()

    pl.semaphore_wait(barrier, expected)

    def row_copies(entries, base):
        rights, lefts = [], []
        for n, (ref, skip, count) in enumerate(entries):
            first = H + ROWS - skip - count
            rights.append(pltpu.make_async_remote_copy(
                src_ref=ref.at[pl.ds(first, count), pl.ds(1, NZ)],
                dst_ref=ref.at[pl.ds(first - ROWS, count), pl.ds(1, NZ)],
                send_sem=fs_send.at[base + n, 0], recv_sem=fs_recv.at[base + n, 0],
                device_id=(t, s + 1), device_id_type=MESH))
            first = H + skip
            lefts.append(pltpu.make_async_remote_copy(
                src_ref=ref.at[pl.ds(first, count), pl.ds(1, NZ)],
                dst_ref=ref.at[pl.ds(first + ROWS, count), pl.ds(1, NZ)],
                send_sem=fs_send.at[base + n, 1], recv_sem=fs_recv.at[base + n, 1],
                device_id=(t, s - 1), device_id_type=MESH))
        return rights, lefts

    def start(copies):
        rights, lefts = copies

        @pl.when(has_right)
        def _():
            for c in rights:
                c.start()

        @pl.when(has_left)
        def _():
            for c in lefts:
                c.start()

    def landed(copies):
        rights, lefts = copies

        @pl.when(has_left)
        def _():
            for c in rights:
                c.wait_recv()

        @pl.when(has_right)
        def _():
            for c in lefts:
                c.wait_recv()

    def sent(copies):
        rights, lefts = copies

        @pl.when(has_right)
        def _():
            for c in rights:
                c.wait_send()

        @pl.when(has_left)
        def _():
            for c in lefts:
                c.wait_send()

    def coarse_copy(src, dst, reach, dt, base, ds):
        j = reach - ds
        return pltpu.make_async_remote_copy(
            src_ref=src, dst_ref=dst.at[j], send_sem=cs_send.at[base + j], recv_sem=cs_recv.at[base + j],
            device_id=(t + dt, s + ds), device_id_type=MESH)

    def each_target(src, dst, reach, dt, base, action):
        def one(j, _):
            ds = j - reach
            ok = there(dt, ds)
            if dt == 0:
                ok = ok & (ds != 0)

            @pl.when(ok)
            def _():
                c = coarse_copy(src, dst, reach, dt, base, ds)
                c.start() if action == "start" else c.wait_send()

            return 0
        lax.fori_loop(0, 2 * reach + 1, one, 0)

    def each_source(src, dst, reach, dt, base):
        def one(j, _):
            ds = reach - j
            ok = there(-dt, -ds)
            if dt == 0:
                ok = ok & (ds != 0)

            @pl.when(ok)
            def _():
                coarse_copy(src, dst, reach, dt, base, ds).wait_recv()

            return 0
        lax.fori_loop(0, 2 * reach + 1, one, 0)

    def inside(row):
        return ((row >= 0) & (row < SPACE * ROWS)).astype(F32)

    def over(rows, body):
        lo, hi = rows

        def one(j, _):
            body(lo + lax.div(j, BLOCKS), U * lax.rem(j, BLOCKS))
            return 0
        lax.fori_loop(0, (hi - lo) * BLOCKS, one, 0)

    def six(ref, e, z0):
        mid = ref[e, pl.ds(z0, U + 2)]
        return ref[e - 1, pl.ds(z0 + 1, U)], ref[e + 1, pl.ds(z0 + 1, U)], mid

    def advance(c, new_c, f, e, z0, which, full):
        cxm, cxp, cz = six(c, e, z0)
        uxm, uxp, uz = six(u.at[0], e, z0)
        c0, u0 = cz[1:-1], uz[1:-1]
        cym, cyp = prev_y(c0, masks), next_y(c0, masks)
        w = u[1, e, pl.ds(z0, U + 2)]
        v = u[2, e, pl.ds(z0 + 1, U)]
        vm, vp = prev_y(v, masks), next_y(v, masks)
        net = upwind(c0, cxp, u0, uxp) - upwind(cxm, c0, uxm, u0)
        fz = upwind(cz[:-1], cz[1:], w[:-1], w[1:])
        net = net + (fz[1:] - fz[:-1])
        net = net + (upwind(c0, cyp, v, vp) - upwind(cym, c0, vm, v))
        fresh = c0 - 0.125 * net
        pull = elec[f, which] * wall[pl.ds(z0, U)] / rho_of(c0)
        around = uxm + uxp + uz[:-2] + uz[2:] + prev_y(u0, masks) + next_y(u0, masks)
        px = 0.85 * u0 + (0.025 * around + pull * (cxp - cxm))
        if not full:
            keep = inside(first_row + e - H)
            fresh = fresh * keep
            px = px * keep
        new_c[e, pl.ds(z0 + 1, U)] = fresh
        pv[0, e, pl.ds(z0 + 1, U)] = px
        if full:
            wxm, wxp = u[1, e - 1, pl.ds(z0 + 1, U)], u[1, e + 1, pl.ds(z0 + 1, U)]
            w0_ = w[1:-1]
            around = wxm + wxp + w[:-2] + w[2:] + prev_y(w0_, masks) + next_y(w0_, masks)
            pv[1, e, pl.ds(z0 + 1, U)] = 0.85 * w0_ + (0.025 * around + pull * (cz[2:] - cz[:-2]))
            vxm, vxp, vz = six(u.at[2], e, z0)
            around = vxm + vxp + vz[:-2] + vz[2:] + vm + vp
            pv[2, e, pl.ds(z0 + 1, U)] = 0.85 * v + (0.025 * around + pull * (cyp - cym))

    def face_block(new_c, e, z0, top):
        rz = rho_of(new_c[e, pl.ds(z0, U + 2)])
        r0 = rz[1:-1]
        rxm = rho_of(new_c[e - 1, pl.ds(z0 + 1, U)])
        rxp = rho_of(new_c[e + 1, pl.ds(z0 + 1, U)])
        lower = 1.0 / (rxm + r0)
        upper = 1.0 / (rxp + r0)
        gx[e, pl.ds(z0, U)] = lower
        gx[e + 1, pl.ds(z0, U)] = upper
        zface = 1.0 / (rz[:-1] + rz[1:])
        gz[e, pl.ds(z0, U + 1)] = zface
        yl = 1.0 / (r0 + prev_y(r0, masks, 0.1))
        yu = 1.0 / (r0 + next_y(r0, masks, 0.1))
        gyl[e, pl.ds(z0, U)] = yl
        gyu[e, pl.ds(z0, U)] = yu
        total = lower + upper + (zface[:-1] + zface[1:]) + (yl + yu)
        inverse = 1.0 / total
        if not top:
            inverse = inverse * inside(first_row + e - H)
        rt[e, pl.ds(z0, U)] = inverse
        return inverse

    def first_pressure(new_c, e, z0):
        inverse = face_block(new_c, e, z0, True)
        pz = pv[1, e, pl.ds(z0, U + 2)]
        py = pv[2, e, pl.ds(z0 + 1, U)]
        source = pv[0, e + 1, pl.ds(z0 + 1, U)] - pv[0, e - 1, pl.ds(z0 + 1, U)]
        source = source + (pz[2:] - pz[:-2]) + (next_y(py, masks) - prev_y(py, masks))
        p1[e, pl.ds(z0 + 1, U)] = -(source * inverse)

    def sweep(old, new, e, z0):
        pxm, pxp, pz = six(old, e, z0)
        p0 = pz[1:-1]
        zface = gz[e, pl.ds(z0, U + 1)]
        summed = gx[e, pl.ds(z0, U)] * pxm + gx[e + 1, pl.ds(z0, U)] * pxp
        summed = summed + (zface[:-1] * pz[:-2] + zface[1:] * pz[2:])
        summed = summed + (gyl[e, pl.ds(z0, U)] * prev_y(p0, masks) + gyu[e, pl.ds(z0, U)] * next_y(p0, masks))
        new[e, pl.ds(z0 + 1, U)] = p1[e, pl.ds(z0 + 1, U)] + rt[e, pl.ds(z0, U)] * summed

    def project(new_c, e, z0):
        pxm, pxp, pz = six(p_a, e, z0)
        p0 = pz[1:-1]
        scale = 0.125 / rho_of(new_c[e, pl.ds(z0 + 1, U)])
        zs = pl.ds(z0 + 1, U)
        u[0, e, zs] = pv[0, e, zs] - scale * (pxp - pxm)
        u[1, e, zs] = pv[1, e, zs] - scale * (pz[2:] - pz[:-2])
        u[2, e, zs] = pv[2, e, zs] - scale * (next_y(p0, masks) - prev_y(p0, masks))

    even, low = lax.rem(lane, 2) == 0, lax.rem(lane, 4) < 2
    spread = jnp.where(lax.rem(lane, 4) == 0, fraction_spread, velocity_spread).astype(F32)

    def combine(a, b, by, mask):
        keep, other = jnp.where(mask, a, b), jnp.where(mask, b, a)
        return keep + jnp.where(mask, roll(other, LANE - by, 1), roll(other, by, 1))

    def restrict(c, out):
        def one(zc, _):
            sums = []
            for ref in (c, u.at[0], u.at[1], u.at[2]):
                total = None
                for i in range(ROWS):
                    part = ref[H + i, pl.ds(1 + 4 * zc, 4)]
                    total = part if total is None else total + part
                sums.append((total[0] + total[1]) + (total[2] + total[3]))
            pair = combine(sums[0], sums[1], 1, even), combine(sums[2], sums[3], 1, even)
            out[zc] = combine(pair[0], pair[1], 2, low) * (1.0 / 64.0)
            return 0
        lax.fori_loop(0, 4, one, 0)

    def diffuse(src, dst, length, out_reach):
        def one(j, _):
            v = src[j + 1]
            up = jnp.concatenate([v[1:], zero_line[None]], axis=0)
            down = jnp.concatenate([zero_line[None], v[:-1]], axis=0)
            around = src[j] + src[j + 2] + up + down + next_y(v, masks, by=4) + prev_y(v, masks, by=4)
            row = s + j - out_reach
            keep = ((row >= 0) & (row < SPACE)).astype(F32)
            dst[j] = (v + spread * (around - 6.0 * v)) * keep
            return 0
        lax.fori_loop(0, length, one, 0)

    def diffuse_down(src, reach, steps):
        now = src
        for step in range(steps):
            reach -= 1
            target = w0 if step % 2 == 0 else w1
            diffuse(now, target, 2 * reach + 1, reach)
            now = target
        return now

    first = row_copies([(c_a, 0, 2), (u.at[0], 0, 2), (u.at[1], 0, 1), (u.at[2], 0, 1)], 0)
    start(first)
    restrict(c_a, cstart.at[2])
    each_target(cstart.at[2], cstart, 2, 0, 0, "start")

    pending = [first]
    c, new_c = c_a, c_b
    for f in range(FINE):
        round_in = pending[-1]
        over((H + 1, H + ROWS - 1), lambda e, z0: advance(c, new_c, f, e, z0, 1, True))
        landed(round_in)
        over((H, H + 1), lambda e, z0: advance(c, new_c, f, e, z0, 1, True))
        over((H + ROWS - 1, H + ROWS), lambda e, z0: advance(c, new_c, f, e, z0, 1, True))
        fraction_rows = row_copies([(new_c, 1, 3)], 4 + 6 * f)
        start(fraction_rows)
        over((H - 1, H), lambda e, z0: advance(c, new_c, f, e, z0, 0, False))
        over((H + ROWS, H + ROWS + 1), lambda e, z0: advance(c, new_c, f, e, z0, 2, False))
        over((H, H + ROWS), lambda e, z0: first_pressure(new_c, e, z0))
        pressure_rows = row_copies([(p1, 0, 4)], 5 + 6 * f)
        start(pressure_rows)
        if f == 0:
            each_source(cstart.at[2], cstart, 2, 0, 0)
            done = diffuse_down(cstart, 2, 2)
            prev[...] = done[0] * (t > 0).astype(F32)
        landed(fraction_rows)
        over((1, H), lambda e, z0: face_block(new_c, e, z0, False))
        over((H + ROWS, EXT - 1), lambda e, z0: face_block(new_c, e, z0, False))
        over((H + 1, H + ROWS - 1), lambda e, z0: sweep(p1, p_a, e, z0))
        landed(pressure_rows)
        over((1, H + 1), lambda e, z0: sweep(p1, p_a, e, z0))
        over((H + ROWS - 1, EXT - 1), lambda e, z0: sweep(p1, p_a, e, z0))
        over((2, EXT - 2), lambda e, z0: sweep(p_a, p_b, e, z0))
        over((3, EXT - 3), lambda e, z0: sweep(p_b, p_a, e, z0))
        sent(round_in)
        over((H, H + ROWS), lambda e, z0: project(new_c, e, z0))
        sent(fraction_rows)
        sent(pressure_rows)
        if f == 0:
            again = row_copies([(u.at[0], 0, 2), (u.at[1], 0, 1), (u.at[2], 0, 1)], 6)
            start(again)
            pending.append(again)
        c, new_c = new_c, c
    each_target(cstart.at[2], cstart, 2, 0, 0, "sent")

    restrict(c, drive)
    drive[...] = drive[...] - prev[...]
    each_target(drive, rx1, 2, 1, 5, "start")
    each_target(drive, rx2, 4, 2, 10, "start")
    each_source(drive, rx2, 4, 2, 10)
    two = diffuse_down(rx2, 4, 2)
    each_source(drive, rx1, 2, 1, 5)

    def join(j, _):
        two[j] = two[j] + rx1[j]
        return 0
    lax.fori_loop(0, 5, join, 0)
    diffuse(two, w0, 3, 1)
    diffuse(w0, w1, 1, 0)
    t1[...] = w1[0]
    each_target(t1, rxs, 4, 2, 19, "start")
    each_source(t1, rxs, 4, 2, 19)
    t2[...] = t1[...] + diffuse_down(rxs, 4, 4)[0]
    each_target(t2, rxq, 8, 4, 28, "start")
    each_source(t2, rxq, 8, 4, 28)
    correction = (t2[...] + diffuse_down(rxq, 8, 8)[0]) - prev[...]
    w0[0] = correction

    stores = []
    for field in range(4):
        target = c if field == 0 else u.at[field - 1]

        def correct(zc, _, field=field, target=target):
            m = jnp.where(lax.rem(lane, 4) == field, w0[0, zc], 0.0)
            m = m + roll(m, 1 if field % 2 == 0 else LANE - 1, 1)
            m = m + roll(m, 2 if field < 2 else LANE - 2, 1)
            for i in range(ROWS):
                zs = pl.ds(1 + 4 * zc, 4)
                target[H + i, zs] = target[H + i, zs] + m[None]
            return 0
        lax.fori_loop(0, 4, correct, 0)
        for k in range(SUB):
            cols = pl.ds(LANE * k, LANE)
            home = ofrac_ref.at[0, :, :, cols] if field == 0 else ovel_ref.at[0, field - 1, :, :, cols]
            stores.append(pltpu.make_async_copy(
                target.at[pl.ds(H, ROWS), pl.ds(1, NZ), k, :], home, out_sem.at[field, k]))
            stores[-1].start()
    each_target(drive, rx1, 2, 1, 5, "sent")
    each_target(drive, rx2, 4, 2, 10, "sent")
    each_target(t1, rxs, 4, 2, 19, "sent")
    each_target(t2, rxq, 8, 4, 28, "sent")
    for c_ in stores:
        c_.wait()


def shards(fraction_levels, start_velocity, electrode_plan):
    line = (SUB, LANE)
    pad = (EXT, NZ + 2) + line
    flat = (EXT, NZ) + line
    row = (4,) + line

    def vmem(*shape):
        return pltpu.VMEM(shape, F32)

    return pl.pallas_call(
        kernel,
        out_shape=(
            jax.ShapeDtypeStruct(fraction_levels.shape, F32),
            jax.ShapeDtypeStruct(start_velocity.shape, F32),
        ),
        in_specs=[
            pl.BlockSpec(memory_space=pl.ANY),
            pl.BlockSpec(memory_space=pl.ANY),
            pl.BlockSpec(memory_space=pltpu.SMEM),
        ],
        out_specs=(pl.BlockSpec(memory_space=pl.ANY), pl.BlockSpec(memory_space=pl.ANY)),
        scratch_shapes=[
            pltpu.VMEM((ROWS, NZ) + line, jnp.int32),
            vmem(*pad), vmem(*pad),
            vmem(3, *pad), vmem(3, *pad),
            vmem(EXT + 1, NZ, *line), vmem(*pad), vmem(*flat), vmem(*flat), vmem(*flat),
            vmem(*pad), vmem(*pad), vmem(*pad),
            vmem(FINE, 3, *line), vmem(NZ, *line),
            vmem(5, *row), vmem(*row), vmem(*row),
            vmem(5, *row), vmem(9, *row), vmem(9, *row), vmem(17, *row),
            vmem(*row), vmem(*row), vmem(17, *row), vmem(17, *row),
            pltpu.SemaphoreType.DMA((4, SUB)), pltpu.SemaphoreType.DMA((4, SUB)),
            pltpu.SemaphoreType.DMA((12, 2)), pltpu.SemaphoreType.DMA((12, 2)),
            pltpu.SemaphoreType.DMA((45,)), pltpu.SemaphoreType.DMA((45,)),
        ],
        compiler_params=pltpu.CompilerParams(
            collective_id=0, has_side_effects=True, vmem_limit_bytes=48 * 2**20
        ),
    )(fraction_levels, start_velocity, electrode_plan)


def solution(mesh):
    return jax.shard_map(
        shards,
        mesh=mesh,
        in_specs=(
            P("tm", "space", None, None),
            P("tm", None, "space", None, None),
            P("tm", None, None),
        ),
        out_specs=(P("tm", "space", None, None), P("tm", None, "space", None, None)),
        check_vma=False,
    )
```

```python
import functools

import jax
import jax.numpy as jnp
from jax import lax
from jax.experimental import pallas as pl
from jax.experimental.pallas import tpu as pltpu
from jax.sharding import PartitionSpec as P

MESH = pl.DeviceIdType.MESH
F32 = jnp.float32

ROWS = 4
NZ = 16
SUB, LANE = 8, 128
H = 4
EXT = ROWS + 2 * H
TILE = 32
TILES = 4
STRIPS = 32
FINE = 2
U = 16
BLOCKS = NZ // U

SLICES, SPACE = 8, 32
wall_scale = 1.5 * 0.25 * 0.5
wall_decay = 4.0
level_scale = 1.0 / 1024.0
fraction_spread, velocity_spread = 0.05, 0.15


def lane_ids():
    sub = lax.broadcasted_iota(jnp.int32, (SUB, LANE), 0)
    lane = lax.broadcasted_iota(jnp.int32, (SUB, LANE), 1)
    return sub, lane


def roll(v, by, axis):
    return pltpu.roll(v, by, axis)


def next_y(v, masks, fill=0.0, by=1):
    ax = v.ndim
    r = roll(v, LANE - by, ax - 1)
    q = roll(r, SUB - 1, ax - 2)
    if fill is not None:
        q = jnp.where(masks["last_sub"], fill, q)
    return jnp.where(masks["last_lane"] if by == 1 else masks["last_group"], q, r)


def prev_y(v, masks, fill=0.0, by=1):
    ax = v.ndim
    r = roll(v, by, ax - 1)
    q = roll(r, 1, ax - 2)
    if fill is not None:
        q = jnp.where(masks["first_sub"], fill, q)
    return jnp.where(masks["first_lane"] if by == 1 else masks["first_group"], q, r)


def upwind(lower, upper, speed_lower, speed_upper):
    speed = speed_lower + speed_upper
    return speed * jnp.where(speed > 0.0, lower, upper)


def rho_of(c):
    return 0.1 + 0.9 * jnp.clip(c, 0.0, 1.0)


def kernel(
    lev_ref, vel_ref, plan_ref, ofrac_ref, ovel_ref,
    levb, c_a, c_b, u, pv, gx, gz, gyl, gyu, rt, p1, p_a, p_b, elec, wall,
    cstart, prev, drive, rx1, rx2, rxs, rxq, t1, t2, w0, w1,
    in_sem, out_sem, fs_send, fs_recv, cs_send, cs_recv,
):
    t = lax.axis_index("tm")
    s = lax.axis_index("space")
    sub, lane = lane_ids()
    masks = {
        "last_sub": sub == SUB - 1, "first_sub": sub == 0,
        "last_lane": lane == LANE - 1, "first_lane": lane == 0,
        "last_cell": (sub == SUB - 1) & (lane == LANE - 1), "first_cell": (sub == 0) & (lane == 0),
        "last_group": lane >= LANE - 4, "first_group": lane < 4,
    }

    def there(dt, ds):
        return (t + dt >= 0) & (t + dt < SLICES) & (s + ds >= 0) & (s + ds < SPACE)

    has_left, has_right = s > 0, s < SPACE - 1

    loads = []
    for k in range(SUB):
        cols = pl.ds(LANE * k, LANE)
        loads.append(pltpu.make_async_copy(lev_ref.at[0, :, :, cols], levb.at[:, :, k, :], in_sem.at[0, k]))
        for d in range(3):
            loads.append(pltpu.make_async_copy(
                vel_ref.at[0, d, :, :, cols], u.at[d, pl.ds(H, ROWS), pl.ds(1, NZ), k, :], in_sem.at[1 + d, k]))
    for c in loads:
        c.start()

    zero_line = jnp.zeros((SUB, LANE), F32)

    def zero_pads(e, _):
        for ref in (c_a, c_b, p1, p_a, p_b, pv.at[1], u.at[0], u.at[1], u.at[2]):
            ref[e, 0] = zero_line
            ref[e, NZ + 1] = zero_line
        return 0

    lax.fori_loop(0, EXT, zero_pads, 0)

    def zero_rows(first):
        def one(j, _):
            z = 1 + lax.rem(j, NZ)
            e = first + lax.div(j, NZ)
            for ref in (c_a, c_b, p1, u.at[0], u.at[1], u.at[2]):
                ref[e, z] = zero_line
            return 0
        lax.fori_loop(0, H * NZ, one, 0)

    @pl.when(s == 0)
    def _():
        zero_rows(0)

    @pl.when(s == SPACE - 1)
    def _():
        zero_rows(H + ROWS)

    zero_coarse = jnp.zeros((4, SUB, LANE), F32)
    for ref in (cstart, rx1, rx2, rxs, rxq):
        def one_row(j, _, ref=ref):
            ref[j] = zero_coarse
            return 0
        lax.fori_loop(0, ref.shape[0], one_row, 0)

    barrier = pltpu.get_barrier_semaphore()
    groups = [(0, 2)] + [(sign * k, r) for k, r in ((1, 2), (2, 4), (4, 8)) for sign in (1, -1)]
    expected = jnp.int32(0)
    for dt, reach in groups:
        def greet(j, count, dt=dt, reach=reach):
            ds = j - reach
            ok = there(dt, ds)
            if dt == 0:
                ok = ok & (ds != 0)

            @pl.when(ok)
            def _():
                pl.semaphore_signal(barrier, inc=1, device_id=(t + dt, s + ds), device_id_type=MESH)

            return count + ok.astype(jnp.int32)
        expected = lax.fori_loop(0, 2 * reach + 1, greet, expected)

    strip = sub * 4 + lax.div(lane, TILE)
    first_row = s * ROWS
    tiles = [jnp.clip(lax.div(first_row - 1 + TILE, TILE) - 1, 0, TILES - 1), lax.div(first_row, TILE),
             jnp.clip(lax.div(first_row + ROWS, TILE), 0, TILES - 1)]
    for f in range(FINE):
        for j, tile in enumerate(tiles):
            def paint(q, field, f=f, tile=tile):
                return jnp.where(strip == q, plan_ref[f, tile, q].astype(F32), field)
            elec[f, j] = lax.fori_loop(0, STRIPS, paint, zero_line)
    for z in range(NZ):
        wall[z] = jnp.full((SUB, LANE), wall_scale, F32) * jnp.exp(jnp.full((SUB, LANE), -z / wall_decay, F32))

    for k in range(SUB):
        loads[4 * k].wait()

    for i in range(ROWS):
        c_a[H + i, pl.ds(1, NZ)] = levb[i].astype(F32) * level_scale

    for k in range(SUB):
        for d in range(3):
            loads[4 * k + 1 + d].wait()

    pl.semaphore_wait(barrier, expected)

    def row_copies(entries, base):
        rights, lefts = [], []
        for n, (ref, skip, count) in enumerate(entries):
            first = H + ROWS - skip - count
            rights.append(pltpu.make_async_remote_copy(
                src_ref=ref.at[pl.ds(first, count), pl.ds(1, NZ)],
                dst_ref=ref.at[pl.ds(first - ROWS, count), pl.ds(1, NZ)],
                send_sem=fs_send.at[base + n, 0], recv_sem=fs_recv.at[base + n, 0],
                device_id=(t, s + 1), device_id_type=MESH))
            first = H + skip
            lefts.append(pltpu.make_async_remote_copy(
                src_ref=ref.at[pl.ds(first, count), pl.ds(1, NZ)],
                dst_ref=ref.at[pl.ds(first + ROWS, count), pl.ds(1, NZ)],
                send_sem=fs_send.at[base + n, 1], recv_sem=fs_recv.at[base + n, 1],
                device_id=(t, s - 1), device_id_type=MESH))
        return rights, lefts

    def start(copies):
        rights, lefts = copies

        @pl.when(has_right)
        def _():
            for c in rights:
                c.start()

        @pl.when(has_left)
        def _():
            for c in lefts:
                c.start()

    def landed(copies):
        rights, lefts = copies

        @pl.when(has_left)
        def _():
            for c in rights:
                c.wait_recv()

        @pl.when(has_right)
        def _():
            for c in lefts:
                c.wait_recv()

    def sent(copies):
        rights, lefts = copies

        @pl.when(has_right)
        def _():
            for c in rights:
                c.wait_send()

        @pl.when(has_left)
        def _():
            for c in lefts:
                c.wait_send()

    def coarse_copy(src, dst, reach, dt, base, ds):
        j = reach - ds
        return pltpu.make_async_remote_copy(
            src_ref=src, dst_ref=dst.at[j], send_sem=cs_send.at[base + j], recv_sem=cs_recv.at[base + j],
            device_id=(t + dt, s + ds), device_id_type=MESH)

    def each_target(src, dst, reach, dt, base, action):
        def one(j, _):
            ds = j - reach
            ok = there(dt, ds)
            if dt == 0:
                ok = ok & (ds != 0)

            @pl.when(ok)
            def _():
                c = coarse_copy(src, dst, reach, dt, base, ds)
                c.start() if action == "start" else c.wait_send()

            return 0
        lax.fori_loop(0, 2 * reach + 1, one, 0)

    def each_source(src, dst, reach, dt, base):
        def one(j, _):
            ds = reach - j
            ok = there(-dt, -ds)
            if dt == 0:
                ok = ok & (ds != 0)

            @pl.when(ok)
            def _():
                coarse_copy(src, dst, reach, dt, base, ds).wait_recv()

            return 0
        lax.fori_loop(0, 2 * reach + 1, one, 0)

    def inside(row):
        return ((row >= 0) & (row < SPACE * ROWS)).astype(F32)

    def over(rows, body):
        lo, hi = rows

        def one(j, _):
            body(lo + lax.div(j, BLOCKS), U * lax.rem(j, BLOCKS))
            return 0
        lax.fori_loop(0, (hi - lo) * BLOCKS, one, 0)

    def six(ref, e, z0):
        mid = ref[e, pl.ds(z0, U + 2)]
        return ref[e - 1, pl.ds(z0 + 1, U)], ref[e + 1, pl.ds(z0 + 1, U)], mid

    def advance(c, new_c, f, e, z0, which, full):
        cxm, cxp, cz = six(c, e, z0)
        uxm, uxp, uz = six(u.at[0], e, z0)
        c0, u0 = cz[1:-1], uz[1:-1]
        cym, cyp = prev_y(c0, masks), next_y(c0, masks)
        w = u[1, e, pl.ds(z0, U + 2)]
        v = u[2, e, pl.ds(z0 + 1, U)]
        vm, vp = prev_y(v, masks), next_y(v, masks)
        net = upwind(c0, cxp, u0, uxp) - upwind(cxm, c0, uxm, u0)
        fz = upwind(cz[:-1], cz[1:], w[:-1], w[1:])
        net = net + (fz[1:] - fz[:-1])
        net = net + (upwind(c0, cyp, v, vp) - upwind(cym, c0, vm, v))
        fresh = c0 - 0.125 * net
        pull = elec[f, which] * wall[pl.ds(z0, U)] / rho_of(c0)
        around = uxm + uxp + uz[:-2] + uz[2:] + prev_y(u0, masks) + next_y(u0, masks)
        px = 0.85 * u0 + (0.025 * around + pull * (cxp - cxm))
        if not full:
            keep = inside(first_row + e - H)
            fresh = fresh * keep
            px = px * keep
        new_c[e, pl.ds(z0 + 1, U)] = fresh
        pv[0, e, pl.ds(z0 + 1, U)] = px
        if full:
            wxm, wxp = u[1, e - 1, pl.ds(z0 + 1, U)], u[1, e + 1, pl.ds(z0 + 1, U)]
            w0_ = w[1:-1]
            around = wxm + wxp + w[:-2] + w[2:] + prev_y(w0_, masks) + next_y(w0_, masks)
            pv[1, e, pl.ds(z0 + 1, U)] = 0.85 * w0_ + (0.025 * around + pull * (cz[2:] - cz[:-2]))
            vxm, vxp, vz = six(u.at[2], e, z0)
            around = vxm + vxp + vz[:-2] + vz[2:] + vm + vp
            pv[2, e, pl.ds(z0 + 1, U)] = 0.85 * v + (0.025 * around + pull * (cyp - cym))

    def face_block(new_c, e, z0, top):
        rz = rho_of(new_c[e, pl.ds(z0, U + 2)])
        r0 = rz[1:-1]
        rxm = rho_of(new_c[e - 1, pl.ds(z0 + 1, U)])
        rxp = rho_of(new_c[e + 1, pl.ds(z0 + 1, U)])
        lower = 1.0 / (rxm + r0)
        upper = 1.0 / (rxp + r0)
        gx[e, pl.ds(z0, U)] = lower
        gx[e + 1, pl.ds(z0, U)] = upper
        zface = 1.0 / (rz[:-1] + rz[1:])
        gz[e, pl.ds(z0, U + 1)] = zface
        yl = 1.0 / (r0 + prev_y(r0, masks, 0.1))
        yu = 1.0 / (r0 + next_y(r0, masks, 0.1))
        gyl[e, pl.ds(z0, U)] = jnp.where(masks["first_cell"], 0.0, yl)
        gyu[e, pl.ds(z0, U)] = jnp.where(masks["last_cell"], 0.0, yu)
        total = lower + upper + (zface[:-1] + zface[1:]) + (yl + yu)
        inverse = 1.0 / total
        if not top:
            inverse = inverse * inside(first_row + e - H)
        rt[e, pl.ds(z0, U)] = inverse
        return inverse

    def first_pressure(new_c, e, z0):
        inverse = face_block(new_c, e, z0, True)
        pz = pv[1, e, pl.ds(z0, U + 2)]
        py = pv[2, e, pl.ds(z0 + 1, U)]
        source = pv[0, e + 1, pl.ds(z0 + 1, U)] - pv[0, e - 1, pl.ds(z0 + 1, U)]
        source = source + (pz[2:] - pz[:-2]) + (next_y(py, masks) - prev_y(py, masks))
        p1[e, pl.ds(z0 + 1, U)] = -(source * inverse)

    def sweep(old, new, e, z0):
        pxm, pxp, pz = six(old, e, z0)
        p0 = pz[1:-1]
        zface = gz[e, pl.ds(z0, U + 1)]
        summed = gx[e, pl.ds(z0, U)] * pxm + gx[e + 1, pl.ds(z0, U)] * pxp
        summed = summed + (zface[:-1] * pz[:-2] + zface[1:] * pz[2:])
        summed = summed + (gyl[e, pl.ds(z0, U)] * prev_y(p0, masks, None) + gyu[e, pl.ds(z0, U)] * next_y(p0, masks, None))
        new[e, pl.ds(z0 + 1, U)] = p1[e, pl.ds(z0 + 1, U)] + rt[e, pl.ds(z0, U)] * summed

    def project(new_c, e, z0):
        pxm, pxp, pz = six(p_a, e, z0)
        p0 = pz[1:-1]
        scale = 0.125 / rho_of(new_c[e, pl.ds(z0 + 1, U)])
        zs = pl.ds(z0 + 1, U)
        u[0, e, zs] = pv[0, e, zs] - scale * (pxp - pxm)
        u[1, e, zs] = pv[1, e, zs] - scale * (pz[2:] - pz[:-2])
        u[2, e, zs] = pv[2, e, zs] - scale * (next_y(p0, masks) - prev_y(p0, masks))

    even, low = lax.rem(lane, 2) == 0, lax.rem(lane, 4) < 2
    spread = jnp.where(lax.rem(lane, 4) == 0, fraction_spread, velocity_spread).astype(F32)

    def combine(a, b, by, mask):
        keep, other = jnp.where(mask, a, b), jnp.where(mask, b, a)
        return keep + jnp.where(mask, roll(other, LANE - by, 2), roll(other, by, 2))

    def restrict(c, out):
        sums = []
        for ref in (c, u.at[0], u.at[1], u.at[2]):
            total = None
            for i in range(ROWS):
                part = ref[H + i, pl.ds(1, NZ)]
                total = part if total is None else total + part
            sums.append(jnp.sum(total.reshape(4, 4, SUB, LANE), axis=1))
        pair = combine(sums[0], sums[1], 1, even), combine(sums[2], sums[3], 1, even)
        out[...] = combine(pair[0], pair[1], 2, low) * (1.0 / 64.0)

    def diffuse(src, dst, length, out_reach):
        whole = src[pl.ds(0, length + 2)]
        v = whole[1:-1]
        edge = jnp.zeros((length, 1, SUB, LANE), F32)
        up = jnp.concatenate([v[:, 1:], edge], axis=1)
        down = jnp.concatenate([edge, v[:, :-1]], axis=1)
        around = whole[:-2] + whole[2:] + up + down + next_y(v, masks, by=4) + prev_y(v, masks, by=4)
        fresh = v + spread * (around - 6.0 * v)
        for j in range(length):
            row = s + j - out_reach
            keep = ((row >= 0) & (row < SPACE)).astype(F32)
            dst[j] = fresh[j] * keep

    def diffuse_down(src, reach, steps):
        now = src
        for step in range(steps):
            reach -= 1
            target = w0 if step % 2 == 0 else w1
            diffuse(now, target, 2 * reach + 1, reach)
            now = target
        return now

    first = row_copies([(c_a, 0, 2), (u.at[0], 0, 2), (u.at[1], 0, 1), (u.at[2], 0, 1)], 0)
    start(first)
    restrict(c_a, cstart.at[2])
    each_target(cstart.at[2], cstart, 2, 0, 0, "start")

    pending = [first]
    c, new_c = c_a, c_b
    for f in range(FINE):
        round_in = pending[-1]
        over((H + 1, H + ROWS - 1), lambda e, z0: advance(c, new_c, f, e, z0, 1, True))
        landed(round_in)
        over((H, H + 1), lambda e, z0: advance(c, new_c, f, e, z0, 1, True))
        over((H + ROWS - 1, H + ROWS), lambda e, z0: advance(c, new_c, f, e, z0, 1, True))
        fraction_rows = row_copies([(new_c, 1, 3)], 4 + 6 * f)
        start(fraction_rows)
        over((H - 1, H), lambda e, z0: advance(c, new_c, f, e, z0, 0, False))
        over((H + ROWS, H + ROWS + 1), lambda e, z0: advance(c, new_c, f, e, z0, 2, False))
        over((H, H + ROWS), lambda e, z0: first_pressure(new_c, e, z0))
        pressure_rows = row_copies([(p1, 0, 4)], 5 + 6 * f)
        start(pressure_rows)
        if f == 0:
            each_source(cstart.at[2], cstart, 2, 0, 0)
            done = diffuse_down(cstart, 2, 2)
            prev[...] = done[0] * (t > 0).astype(F32)
        landed(fraction_rows)
        over((1, H), lambda e, z0: face_block(new_c, e, z0, False))
        over((H + ROWS, EXT - 1), lambda e, z0: face_block(new_c, e, z0, False))
        over((H + 1, H + ROWS - 1), lambda e, z0: sweep(p1, p_a, e, z0))
        landed(pressure_rows)
        over((1, H + 1), lambda e, z0: sweep(p1, p_a, e, z0))
        over((H + ROWS - 1, EXT - 1), lambda e, z0: sweep(p1, p_a, e, z0))
        over((2, EXT - 2), lambda e, z0: sweep(p_a, p_b, e, z0))
        over((3, EXT - 3), lambda e, z0: sweep(p_b, p_a, e, z0))
        sent(round_in)
        over((H, H + ROWS), lambda e, z0: project(new_c, e, z0))
        sent(fraction_rows)
        sent(pressure_rows)
        if f == 0:
            again = row_copies([(u.at[0], 0, 2), (u.at[1], 0, 1), (u.at[2], 0, 1)], 6)
            start(again)
            pending.append(again)
        c, new_c = new_c, c
    each_target(cstart.at[2], cstart, 2, 0, 0, "sent")

    restrict(c, drive)
    drive[...] = drive[...] - prev[...]
    each_target(drive, rx1, 2, 1, 5, "start")
    each_target(drive, rx2, 4, 2, 10, "start")
    each_source(drive, rx2, 4, 2, 10)
    two = diffuse_down(rx2, 4, 2)
    each_source(drive, rx1, 2, 1, 5)

    two[pl.ds(0, 5)] = two[pl.ds(0, 5)] + rx1[...]
    diffuse(two, w0, 3, 1)
    diffuse(w0, w1, 1, 0)
    t1[...] = w1[0]
    each_target(t1, rxs, 4, 2, 19, "start")
    each_source(t1, rxs, 4, 2, 19)
    t2[...] = t1[...] + diffuse_down(rxs, 4, 4)[0]
    each_target(t2, rxq, 8, 4, 28, "start")
    each_source(t2, rxq, 8, 4, 28)
    correction = (t2[...] + diffuse_down(rxq, 8, 8)[0]) - prev[...]

    stores = []
    for field in range(4):
        target = c if field == 0 else u.at[field - 1]

        m = jnp.where(lax.rem(lane, 4) == field, correction, 0.0)
        m = m + roll(m, 1 if field % 2 == 0 else LANE - 1, 2)
        m = m + roll(m, 2 if field < 2 else LANE - 2, 2)
        m = jnp.broadcast_to(m[:, None], (4, 4, SUB, LANE)).reshape(NZ, SUB, LANE)
        for i in range(ROWS):
            target[H + i, pl.ds(1, NZ)] = target[H + i, pl.ds(1, NZ)] + m
        for k in range(SUB):
            cols = pl.ds(LANE * k, LANE)
            home = ofrac_ref.at[0, :, :, cols] if field == 0 else ovel_ref.at[0, field - 1, :, :, cols]
            stores.append(pltpu.make_async_copy(
                target.at[pl.ds(H, ROWS), pl.ds(1, NZ), k, :], home, out_sem.at[field, k]))
            stores[-1].start()
    each_target(drive, rx1, 2, 1, 5, "sent")
    each_target(drive, rx2, 4, 2, 10, "sent")
    each_target(t1, rxs, 4, 2, 19, "sent")
    each_target(t2, rxq, 8, 4, 28, "sent")
    for c_ in stores:
        c_.wait()


def shards(fraction_levels, start_velocity, electrode_plan):
    line = (SUB, LANE)
    pad = (EXT, NZ + 2) + line
    flat = (EXT, NZ) + line
    row = (4,) + line

    def vmem(*shape):
        return pltpu.VMEM(shape, F32)

    return pl.pallas_call(
        kernel,
        out_shape=(
            jax.ShapeDtypeStruct(fraction_levels.shape, F32),
            jax.ShapeDtypeStruct(start_velocity.shape, F32),
        ),
        in_specs=[
            pl.BlockSpec(memory_space=pl.ANY),
            pl.BlockSpec(memory_space=pl.ANY),
            pl.BlockSpec(memory_space=pltpu.SMEM),
        ],
        out_specs=(pl.BlockSpec(memory_space=pl.ANY), pl.BlockSpec(memory_space=pl.ANY)),
        scratch_shapes=[
            pltpu.VMEM((ROWS, NZ) + line, jnp.int32),
            vmem(*pad), vmem(*pad),
            vmem(3, *pad), vmem(3, *pad),
            vmem(EXT + 1, NZ, *line), vmem(*pad), vmem(*flat), vmem(*flat), vmem(*flat),
            vmem(*pad), vmem(*pad), vmem(*pad),
            vmem(FINE, 3, *line), vmem(NZ, *line),
            vmem(5, *row), vmem(*row), vmem(*row),
            vmem(5, *row), vmem(9, *row), vmem(9, *row), vmem(17, *row),
            vmem(*row), vmem(*row), vmem(17, *row), vmem(17, *row),
            pltpu.SemaphoreType.DMA((4, SUB)), pltpu.SemaphoreType.DMA((4, SUB)),
            pltpu.SemaphoreType.DMA((12, 2)), pltpu.SemaphoreType.DMA((12, 2)),
            pltpu.SemaphoreType.DMA((45,)), pltpu.SemaphoreType.DMA((45,)),
        ],
        compiler_params=pltpu.CompilerParams(
            collective_id=0, has_side_effects=True, vmem_limit_bytes=62 * 2**20
        ),
    )(fraction_levels, start_velocity, electrode_plan)


def solution(mesh):
    return jax.shard_map(
        shards,
        mesh=mesh,
        in_specs=(
            P("tm", "space", None, None),
            P("tm", None, "space", None, None),
            P("tm", None, None),
        ),
        out_specs=(P("tm", "space", None, None), P("tm", None, "space", None, None)),
        check_vma=False,
    )
```

```python
import functools

import jax
import jax.numpy as jnp
from jax import lax
from jax.experimental import pallas as pl
from jax.experimental.pallas import tpu as pltpu
from jax.sharding import PartitionSpec as P

MESH = pl.DeviceIdType.MESH
F32 = jnp.float32

ROWS = 4
NZ = 16
SUB, LANE = 8, 128
H = 4
EXT = ROWS + 2 * H
TILE = 32
TILES = 4
STRIPS = 32
FINE = 2
U = 16
BLOCKS = NZ // U

SLICES, SPACE = 8, 32
wall_scale = 1.5 * 0.25 * 0.5
wall_decay = 4.0
level_scale = 1.0 / 1024.0
fraction_spread, velocity_spread = 0.05, 0.15


def lane_ids():
    sub = lax.broadcasted_iota(jnp.int32, (SUB, LANE), 0)
    lane = lax.broadcasted_iota(jnp.int32, (SUB, LANE), 1)
    return sub, lane


def roll(v, by, axis):
    return pltpu.roll(v, by, axis)


def next_y(v, masks, fill=0.0, by=1):
    ax = v.ndim
    r = roll(v, LANE - by, ax - 1)
    q = roll(r, SUB - 1, ax - 2)
    if fill is not None:
        q = jnp.where(masks["last_sub"], fill, q)
    return jnp.where(masks["last_lane"] if by == 1 else masks["last_group"], q, r)


def prev_y(v, masks, fill=0.0, by=1):
    ax = v.ndim
    r = roll(v, by, ax - 1)
    q = roll(r, 1, ax - 2)
    if fill is not None:
        q = jnp.where(masks["first_sub"], fill, q)
    return jnp.where(masks["first_lane"] if by == 1 else masks["first_group"], q, r)


def upwind(lower, upper, speed_lower, speed_upper):
    speed = speed_lower + speed_upper
    return speed * jnp.where(speed > 0.0, lower, upper)


def rho_of(c):
    return 0.1 + 0.9 * jnp.clip(c, 0.0, 1.0)


def kernel(
    lev_ref, vel_ref, plan_ref, ofrac_ref, ovel_ref,
    levb, c_a, c_b, u, pv, gx, gz, gyl, gyu, rt, p1, p_a, p_b, elec, wall,
    cstart, prev, drive, rx1, rx2, rx3, rxs, rxq, part, w0, w1,
    in_sem, out_sem, fs_send, fs_recv, cs_send, cs_recv, hand_sem,
):
    t = lax.axis_index("tm")
    s = lax.axis_index("space")
    sub, lane = lane_ids()
    masks = {
        "last_sub": sub == SUB - 1, "first_sub": sub == 0,
        "last_lane": lane == LANE - 1, "first_lane": lane == 0,
        "last_cell": (sub == SUB - 1) & (lane == LANE - 1), "first_cell": (sub == 0) & (lane == 0),
        "last_group": lane >= LANE - 4, "first_group": lane < 4,
    }

    def there(dt, ds):
        return (t + dt >= 0) & (t + dt < SLICES) & (s + ds >= 0) & (s + ds < SPACE)

    has_left, has_right = s > 0, s < SPACE - 1

    loads = []
    for k in range(SUB):
        cols = pl.ds(LANE * k, LANE)
        loads.append(pltpu.make_async_copy(lev_ref.at[0, :, :, cols], levb.at[:, :, k, :], in_sem.at[0, k]))
        for d in range(3):
            loads.append(pltpu.make_async_copy(
                vel_ref.at[0, d, :, :, cols], u.at[d, pl.ds(H, ROWS), pl.ds(1, NZ), k, :], in_sem.at[1 + d, k]))
    for c in loads:
        c.start()

    zero_line = jnp.zeros((SUB, LANE), F32)
    cstart[...] = jnp.zeros(cstart.shape, F32)

    barrier = pltpu.get_barrier_semaphore()
    beside = [(0, 1), (0, -1), (1, 0), (-1, 0)]

    def tell(semaphore, places):
        for dt, ds in places:
            @pl.when(there(dt, ds))
            def _(dt=dt, ds=ds):
                pl.semaphore_signal(semaphore, inc=1, device_id=(t + dt, s + ds), device_id_type=MESH)

    def hear(semaphore, places):
        count = jnp.int32(0)
        for dt, ds in places:
            count = count + there(dt, ds).astype(jnp.int32)

        @pl.when(count > 0)
        def _():
            pl.semaphore_wait(semaphore, count)

    tell(barrier, beside)

    def zero_pads(e, _):
        for ref in (c_a, c_b, p1, p_a, p_b, pv.at[1], u.at[0], u.at[1], u.at[2]):
            ref[e, 0] = zero_line
            ref[e, NZ + 1] = zero_line
        return 0

    def zero_rows(first):
        def one(e, _):
            for ref in (c_a, c_b, p1, u.at[0], u.at[1], u.at[2]):
                ref[e] = jnp.zeros((NZ + 2, SUB, LANE), F32)
            return 0
        lax.fori_loop(first, first + H, one, 0)

    def fill_tables():
        lax.fori_loop(0, EXT, zero_pads, 0)

        @pl.when(s == 0)
        def _():
            zero_rows(0)

        @pl.when(s == SPACE - 1)
        def _():
            zero_rows(H + ROWS)

        for ref in (rx1, rx2, rx3, rxs, rxq):
            ref[...] = jnp.zeros(ref.shape, F32)
        strip = sub * 4 + lax.div(lane, TILE)
        tiles = [jnp.clip(lax.div(first_row - 1 + TILE, TILE) - 1, 0, TILES - 1), lax.div(first_row, TILE),
                 jnp.clip(lax.div(first_row + ROWS, TILE), 0, TILES - 1)]
        for f in range(FINE):
            def paint(q, fields, f=f):
                return tuple(jnp.where(strip == q, plan_ref[f, tile, q].astype(F32), field)
                             for tile, field in zip(tiles, fields))
            painted = lax.fori_loop(0, STRIPS, paint, (zero_line,) * 3, unroll=4)
            for j in range(3):
                elec[f, j] = painted[j]
        for z in range(NZ):
            wall[z] = jnp.full((SUB, LANE), wall_scale, F32) * jnp.exp(jnp.full((SUB, LANE), -z / wall_decay, F32))

    first_row = s * ROWS
    for k in range(SUB):
        loads[4 * k].wait()
    for i in range(ROWS):
        c_a[H + i, pl.ds(1, NZ)] = levb[i].astype(F32) * level_scale

    for k in range(SUB):
        for d in range(3):
            loads[4 * k + 1 + d].wait()

    hear(barrier, beside)

    def row_copies(entries, base):
        rights, lefts = [], []
        for n, (ref, skip, count) in enumerate(entries):
            first = H + ROWS - skip - count
            rights.append(pltpu.make_async_remote_copy(
                src_ref=ref.at[pl.ds(first, count), pl.ds(1, NZ)],
                dst_ref=ref.at[pl.ds(first - ROWS, count), pl.ds(1, NZ)],
                send_sem=fs_send.at[base + n, 0], recv_sem=fs_recv.at[base + n, 0],
                device_id=(t, s + 1), device_id_type=MESH))
            first = H + skip
            lefts.append(pltpu.make_async_remote_copy(
                src_ref=ref.at[pl.ds(first, count), pl.ds(1, NZ)],
                dst_ref=ref.at[pl.ds(first + ROWS, count), pl.ds(1, NZ)],
                send_sem=fs_send.at[base + n, 1], recv_sem=fs_recv.at[base + n, 1],
                device_id=(t, s - 1), device_id_type=MESH))
        return rights, lefts

    def start(copies):
        rights, lefts = copies

        @pl.when(has_right)
        def _():
            for c in rights:
                c.start()

        @pl.when(has_left)
        def _():
            for c in lefts:
                c.start()

    def landed(copies):
        rights, lefts = copies

        @pl.when(has_left)
        def _():
            for c in rights:
                c.wait_recv()

        @pl.when(has_right)
        def _():
            for c in lefts:
                c.wait_recv()

    def sent(copies):
        rights, lefts = copies

        @pl.when(has_right)
        def _():
            for c in rights:
                c.wait_send()

        @pl.when(has_left)
        def _():
            for c in lefts:
                c.wait_send()

    def coarse_copy(link, src, ds):
        dst, reach, dt, base, lo, hi = link
        j = reach - ds
        return pltpu.make_async_remote_copy(
            src_ref=src, dst_ref=dst.at[j], send_sem=cs_send.at[base + j], recv_sem=cs_recv.at[base + j],
            device_id=(t + dt, s + ds), device_id_type=MESH)

    def each_target(link, src, action):
        dst, reach, dt, base, lo, hi = link

        @pl.when((t >= lo) & (t <= hi))
        def _():
            def one(j, _):
                ds = j - reach
                ok = there(dt, ds)
                if dt == 0:
                    ok = ok & (ds != 0)

                @pl.when(ok)
                def _():
                    c = coarse_copy(link, src, ds)
                    c.start() if action == "start" else c.wait_send()

                return 0
            lax.fori_loop(0, 2 * reach + 1, one, 0)

    def each_source(link, src):
        dst, reach, dt, base, lo, hi = link

        @pl.when((t - dt >= lo) & (t - dt <= hi))
        def _():
            def one(j, _):
                ds = reach - j
                ok = there(-dt, -ds)
                if dt == 0:
                    ok = ok & (ds != 0)

                @pl.when(ok)
                def _():
                    coarse_copy(link, src, ds).wait_recv()

                return 0
            lax.fori_loop(0, 2 * reach + 1, one, 0)

    starts = (cstart, 2, 0, 0, 0, SLICES - 1)
    one_back = (rx1, 2, 1, 5, 0, SLICES - 2)
    two_back = (rx2, 4, 2, 10, 0, SLICES - 3)
    three_back = (rx3, 6, 3, 19, 0, 0)
    sum_two = (rxs, 4, 2, 32, 2, 5)
    sum_four = (rxq, 8, 4, 41, 2, 3)

    def inside(row):
        return ((row >= 0) & (row < SPACE * ROWS)).astype(F32)

    def over(rows, body):
        lo, hi = rows

        def one(j, _):
            body(lo + lax.div(j, BLOCKS), U * lax.rem(j, BLOCKS))
            return 0
        lax.fori_loop(0, (hi - lo) * BLOCKS, one, 0)

    def six(ref, e, z0):
        mid = ref[e, pl.ds(z0, U + 2)]
        return ref[e - 1, pl.ds(z0 + 1, U)], ref[e + 1, pl.ds(z0 + 1, U)], mid

    def advance(c, new_c, f, e, z0, which, full):
        cxm, cxp, cz = six(c, e, z0)
        uxm, uxp, uz = six(u.at[0], e, z0)
        c0, u0 = cz[1:-1], uz[1:-1]
        cym, cyp = prev_y(c0, masks), next_y(c0, masks)
        w = u[1, e, pl.ds(z0, U + 2)]
        v = u[2, e, pl.ds(z0 + 1, U)]
        vm, vp = prev_y(v, masks), next_y(v, masks)
        net = upwind(c0, cxp, u0, uxp) - upwind(cxm, c0, uxm, u0)
        fz = upwind(cz[:-1], cz[1:], w[:-1], w[1:])
        net = net + (fz[1:] - fz[:-1])
        net = net + (upwind(c0, cyp, v, vp) - upwind(cym, c0, vm, v))
        fresh = c0 - 0.125 * net
        pull = elec[f, which] * wall[pl.ds(z0, U)] / rho_of(c0)
        around = uxm + uxp + uz[:-2] + uz[2:] + prev_y(u0, masks) + next_y(u0, masks)
        px = 0.85 * u0 + (0.025 * around + pull * (cxp - cxm))
        if not full:
            keep = inside(first_row + e - H)
            fresh = fresh * keep
            px = px * keep
        new_c[e, pl.ds(z0 + 1, U)] = fresh
        pv[0, e, pl.ds(z0 + 1, U)] = px
        if full:
            wxm, wxp = u[1, e - 1, pl.ds(z0 + 1, U)], u[1, e + 1, pl.ds(z0 + 1, U)]
            w0_ = w[1:-1]
            around = wxm + wxp + w[:-2] + w[2:] + prev_y(w0_, masks) + next_y(w0_, masks)
            pv[1, e, pl.ds(z0 + 1, U)] = 0.85 * w0_ + (0.025 * around + pull * (cz[2:] - cz[:-2]))
            vxm, vxp, vz = six(u.at[2], e, z0)
            around = vxm + vxp + vz[:-2] + vz[2:] + vm + vp
            pv[2, e, pl.ds(z0 + 1, U)] = 0.85 * v + (0.025 * around + pull * (cyp - cym))

    def face_block(new_c, e, z0, top):
        rz = rho_of(new_c[e, pl.ds(z0, U + 2)])
        r0 = rz[1:-1]
        rxm = rho_of(new_c[e - 1, pl.ds(z0 + 1, U)])
        rxp = rho_of(new_c[e + 1, pl.ds(z0 + 1, U)])
        lower = 1.0 / (rxm + r0)
        upper = 1.0 / (rxp + r0)
        gx[e, pl.ds(z0, U)] = lower
        gx[e + 1, pl.ds(z0, U)] = upper
        zface = 1.0 / (rz[:-1] + rz[1:])
        gz[e, pl.ds(z0, U + 1)] = zface
        yl = 1.0 / (r0 + prev_y(r0, masks, 0.1))
        yu = 1.0 / (r0 + next_y(r0, masks, 0.1))
        gyl[e, pl.ds(z0, U)] = jnp.where(masks["first_cell"], 0.0, yl)
        gyu[e, pl.ds(z0, U)] = jnp.where(masks["last_cell"], 0.0, yu)
        total = lower + upper + (zface[:-1] + zface[1:]) + (yl + yu)
        inverse = 1.0 / total
        if not top:
            inverse = inverse * inside(first_row + e - H)
        rt[e, pl.ds(z0, U)] = inverse
        return inverse

    def first_pressure(new_c, e, z0):
        inverse = face_block(new_c, e, z0, True)
        pz = pv[1, e, pl.ds(z0, U + 2)]
        py = pv[2, e, pl.ds(z0 + 1, U)]
        source = pv[0, e + 1, pl.ds(z0 + 1, U)] - pv[0, e - 1, pl.ds(z0 + 1, U)]
        source = source + (pz[2:] - pz[:-2]) + (next_y(py, masks) - prev_y(py, masks))
        p1[e, pl.ds(z0 + 1, U)] = -(source * inverse)

    def sweep(old, new, e, z0):
        pxm, pxp, pz = six(old, e, z0)
        p0 = pz[1:-1]
        zface = gz[e, pl.ds(z0, U + 1)]
        summed = gx[e, pl.ds(z0, U)] * pxm + gx[e + 1, pl.ds(z0, U)] * pxp
        summed = summed + (zface[:-1] * pz[:-2] + zface[1:] * pz[2:])
        summed = summed + (gyl[e, pl.ds(z0, U)] * prev_y(p0, masks, None) + gyu[e, pl.ds(z0, U)] * next_y(p0, masks, None))
        new[e, pl.ds(z0 + 1, U)] = p1[e, pl.ds(z0 + 1, U)] + rt[e, pl.ds(z0, U)] * summed

    def project(new_c, e, z0):
        pxm, pxp, pz = six(p_a, e, z0)
        p0 = pz[1:-1]
        scale = 0.125 / rho_of(new_c[e, pl.ds(z0 + 1, U)])
        zs = pl.ds(z0 + 1, U)
        u[0, e, zs] = pv[0, e, zs] - scale * (pxp - pxm)
        u[1, e, zs] = pv[1, e, zs] - scale * (pz[2:] - pz[:-2])
        u[2, e, zs] = pv[2, e, zs] - scale * (next_y(p0, masks) - prev_y(p0, masks))

    even, low = lax.rem(lane, 2) == 0, lax.rem(lane, 4) < 2
    spread = jnp.where(lax.rem(lane, 4) == 0, fraction_spread, velocity_spread).astype(F32)

    def combine(a, b, by, mask):
        keep, other = jnp.where(mask, a, b), jnp.where(mask, b, a)
        return keep + jnp.where(mask, roll(other, LANE - by, 2), roll(other, by, 2))

    def restrict(c, out):
        sums = []
        for ref in (c, u.at[0], u.at[1], u.at[2]):
            total = None
            for i in range(ROWS):
                part = ref[H + i, pl.ds(1, NZ)]
                total = part if total is None else total + part
            sums.append(jnp.sum(total.reshape(4, 4, SUB, LANE), axis=1))
        pair = combine(sums[0], sums[1], 1, even), combine(sums[2], sums[3], 1, even)
        out[...] = combine(pair[0], pair[1], 2, low) * (1.0 / 64.0)

    def diffuse(src, dst, length, out_reach):
        whole = src[pl.ds(0, length + 2)]
        v = whole[1:-1]
        edge = jnp.zeros((length, 1, SUB, LANE), F32)
        up = jnp.concatenate([v[:, 1:], edge], axis=1)
        down = jnp.concatenate([edge, v[:, :-1]], axis=1)
        around = whole[:-2] + whole[2:] + up + down + next_y(v, masks, by=4) + prev_y(v, masks, by=4)
        fresh = v + spread * (around - 6.0 * v)
        for j in range(length):
            row = s + j - out_reach
            keep = ((row >= 0) & (row < SPACE)).astype(F32)
            dst[j] = fresh[j] * keep

    def diffuse_down(src, reach, steps):
        now = src
        for step in range(steps):
            reach -= 1
            target = w0 if step % 2 == 0 else w1
            diffuse(now, target, 2 * reach + 1, reach)
            now = target
        return now

    first = row_copies([(c_a, 0, 2), (u.at[0], 0, 2), (u.at[1], 0, 1), (u.at[2], 0, 1)], 0)
    start(first)
    tell(hand_sem.at[0], [(1, 0), (-1, 0)])
    fill_tables()
    restrict(c_a, cstart.at[2])

    pending = [first]
    c, new_c = c_a, c_b
    for f in range(FINE):
        round_in = pending[-1]
        over((H + 1, H + ROWS - 1), lambda e, z0: advance(c, new_c, f, e, z0, 1, True))
        landed(round_in)
        if f == 0:
            each_target(starts, cstart.at[2], "start")
            hear(hand_sem.at[0], [(1, 0), (-1, 0)])
            tell(hand_sem.at[1], [(2, 0), (-2, 0)])
        else:
            hear(hand_sem.at[1], [(2, 0), (-2, 0)])
            tell(hand_sem.at[2], [(0, 4), (0, -4)])
        over((H, H + 1), lambda e, z0: advance(c, new_c, f, e, z0, 1, True))
        over((H + ROWS - 1, H + ROWS), lambda e, z0: advance(c, new_c, f, e, z0, 1, True))
        fraction_rows = row_copies([(new_c, 1, 3)], 4 + 6 * f)
        start(fraction_rows)
        over((H - 1, H), lambda e, z0: advance(c, new_c, f, e, z0, 0, False))
        over((H + ROWS, H + ROWS + 1), lambda e, z0: advance(c, new_c, f, e, z0, 2, False))
        over((H, H + ROWS), lambda e, z0: first_pressure(new_c, e, z0))
        pressure_rows = row_copies([(p1, 0, 4)], 5 + 6 * f)
        start(pressure_rows)
        if f == 0:
            each_source(starts, cstart.at[2])
            done = diffuse_down(cstart, 2, 2)
            prev[...] = done[0] * (t > 0).astype(F32)
        landed(fraction_rows)
        if f == 1:
            hear(hand_sem.at[2], [(0, 4), (0, -4)])
            tell(hand_sem.at[3], [(-k, 0) for k in (1, 2, 3, 4)])
        over((1, H), lambda e, z0: face_block(new_c, e, z0, False))
        over((H + ROWS, EXT - 1), lambda e, z0: face_block(new_c, e, z0, False))
        over((H + 1, H + ROWS - 1), lambda e, z0: sweep(p1, p_a, e, z0))
        landed(pressure_rows)
        over((1, H + 1), lambda e, z0: sweep(p1, p_a, e, z0))
        over((H + ROWS - 1, EXT - 1), lambda e, z0: sweep(p1, p_a, e, z0))
        over((2, EXT - 2), lambda e, z0: sweep(p_a, p_b, e, z0))
        over((3, EXT - 3), lambda e, z0: sweep(p_b, p_a, e, z0))
        sent(round_in)
        over((H, H + ROWS), lambda e, z0: project(new_c, e, z0))
        sent(fraction_rows)
        sent(pressure_rows)
        if f == 0:
            again = row_copies([(u.at[0], 0, 2), (u.at[1], 0, 1), (u.at[2], 0, 1)], 6)
            start(again)
            pending.append(again)
        c, new_c = new_c, c
    each_target(starts, cstart.at[2], "sent")

    restrict(c, drive)
    drive[...] = drive[...] - prev[...]
    hear(hand_sem.at[3], [(k, 0) for k in (1, 2, 3, 4)])
    each_target(three_back, drive, "start")
    each_target(two_back, drive, "start")
    each_target(one_back, drive, "start")
    each_source(three_back, drive)
    three = diffuse_down(rx3, 6, 2)
    each_source(two_back, drive)
    three[pl.ds(0, 9)] = three[pl.ds(0, 9)] + rx2[...]
    diffuse(three, w0, 7, 3)
    diffuse(w0, w1, 5, 2)
    each_source(one_back, drive)
    w1[pl.ds(0, 5)] = w1[pl.ds(0, 5)] + rx1[...]
    diffuse(w1, w0, 3, 1)
    diffuse(w0, w1, 1, 0)
    part[...] = w1[0]
    each_target(sum_four, part, "start")
    each_target(sum_two, part, "start")
    each_source(sum_four, part)
    eight = diffuse_down(rxq, 8, 4)
    each_source(sum_two, part)
    eight[pl.ds(0, 9)] = eight[pl.ds(0, 9)] + rxs[...]
    four = diffuse_down(eight, 4, 4)
    correction = (part[...] + four[0]) - prev[...]

    stores = []
    for field in range(4):
        target = c if field == 0 else u.at[field - 1]

        m = jnp.where(lax.rem(lane, 4) == field, correction, 0.0)
        m = m + roll(m, 1 if field % 2 == 0 else LANE - 1, 2)
        m = m + roll(m, 2 if field < 2 else LANE - 2, 2)
        m = jnp.broadcast_to(m[:, None], (4, 4, SUB, LANE)).reshape(NZ, SUB, LANE)
        for i in range(ROWS):
            target[H + i, pl.ds(1, NZ)] = target[H + i, pl.ds(1, NZ)] + m
        for k in range(SUB):
            cols = pl.ds(LANE * k, LANE)
            home = ofrac_ref.at[0, :, :, cols] if field == 0 else ovel_ref.at[0, field - 1, :, :, cols]
            stores.append(pltpu.make_async_copy(
                target.at[pl.ds(H, ROWS), pl.ds(1, NZ), k, :], home, out_sem.at[field, k]))
            stores[-1].start()
    each_target(three_back, drive, "sent")
    each_target(two_back, drive, "sent")
    each_target(one_back, drive, "sent")
    each_target(sum_four, part, "sent")
    each_target(sum_two, part, "sent")
    for c_ in stores:
        c_.wait()


def shards(fraction_levels, start_velocity, electrode_plan):
    line = (SUB, LANE)
    pad = (EXT, NZ + 2) + line
    flat = (EXT, NZ) + line
    row = (4,) + line

    def vmem(*shape):
        return pltpu.VMEM(shape, F32)

    return pl.pallas_call(
        kernel,
        out_shape=(
            jax.ShapeDtypeStruct(fraction_levels.shape, F32),
            jax.ShapeDtypeStruct(start_velocity.shape, F32),
        ),
        in_specs=[
            pl.BlockSpec(memory_space=pl.ANY),
            pl.BlockSpec(memory_space=pl.ANY),
            pl.BlockSpec(memory_space=pltpu.SMEM),
        ],
        out_specs=(pl.BlockSpec(memory_space=pl.ANY), pl.BlockSpec(memory_space=pl.ANY)),
        scratch_shapes=[
            pltpu.VMEM((ROWS, NZ) + line, jnp.int32),
            vmem(*pad), vmem(*pad),
            vmem(3, *pad), vmem(3, *pad),
            vmem(EXT + 1, NZ, *line), vmem(*pad), vmem(*flat), vmem(*flat), vmem(*flat),
            vmem(*pad), vmem(*pad), vmem(*pad),
            vmem(FINE, 3, *line), vmem(NZ, *line),
            vmem(5, *row), vmem(*row), vmem(*row),
            vmem(5, *row), vmem(9, *row), vmem(13, *row), vmem(9, *row), vmem(17, *row),
            vmem(*row), vmem(17, *row), vmem(17, *row),
            pltpu.SemaphoreType.DMA((4, SUB)), pltpu.SemaphoreType.DMA((4, SUB)),
            pltpu.SemaphoreType.DMA((12, 2)), pltpu.SemaphoreType.DMA((12, 2)),
            pltpu.SemaphoreType.DMA((58,)), pltpu.SemaphoreType.DMA((58,)),
            pltpu.SemaphoreType.REGULAR((4,)),
        ],
        compiler_params=pltpu.CompilerParams(
            collective_id=0, has_side_effects=True, vmem_limit_bytes=62 * 2**20
        ),
    )(fraction_levels, start_velocity, electrode_plan)


def solution(mesh):
    return jax.shard_map(
        shards,
        mesh=mesh,
        in_specs=(
            P("tm", "space", None, None),
            P("tm", None, "space", None, None),
            P("tm", None, None),
        ),
        out_specs=(P("tm", "space", None, None), P("tm", None, "space", None, None)),
        check_vma=False,
    )
```

```python
import functools

import jax
import jax.numpy as jnp
from jax import lax
from jax.experimental import pallas as pl
from jax.experimental.pallas import tpu as pltpu
from jax.sharding import PartitionSpec as P

MESH = pl.DeviceIdType.MESH
F32 = jnp.float32

ROWS = 4
NZ = 16
SUB, LANE = 8, 128
H = 4
EXT = ROWS + 2 * H
TILE = 32
TILES = 4
STRIPS = 32
FINE = 2
U = 16
BLOCKS = NZ // U

SLICES, SPACE = 8, 32
wall_scale = 1.5 * 0.25 * 0.5
wall_decay = 4.0
level_scale = 1.0 / 1024.0
fraction_spread, velocity_spread = 0.05, 0.15


def lane_ids():
    sub = lax.broadcasted_iota(jnp.int32, (SUB, LANE), 0)
    lane = lax.broadcasted_iota(jnp.int32, (SUB, LANE), 1)
    return sub, lane


def roll(v, by, axis):
    return pltpu.roll(v, by, axis)


def next_y(v, masks, fill=0.0, by=1):
    ax = v.ndim
    r = roll(v, LANE - by, ax - 1)
    q = roll(r, SUB - 1, ax - 2)
    if fill is not None:
        q = jnp.where(masks["last_sub"], fill, q)
    return jnp.where(masks["last_lane"] if by == 1 else masks["last_group"], q, r)


def prev_y(v, masks, fill=0.0, by=1):
    ax = v.ndim
    r = roll(v, by, ax - 1)
    q = roll(r, 1, ax - 2)
    if fill is not None:
        q = jnp.where(masks["first_sub"], fill, q)
    return jnp.where(masks["first_lane"] if by == 1 else masks["first_group"], q, r)


def upwind(lower, upper, speed_lower, speed_upper):
    speed = speed_lower + speed_upper
    return speed * jnp.where(speed > 0.0, lower, upper)


def rho_of(c):
    return 0.1 + 0.9 * jnp.clip(c, 0.0, 1.0)


def kernel(
    lev_ref, vel_ref, plan_ref, ofrac_ref, ovel_ref,
    levb, c_a, c_b, u, pv, gx, gz, gyl, gyu, rt, p1, p_a, p_b, elec, wall,
    cstart, prev, drive, rx1, rx2, rx3, rxs, rxq, part, w0, w1,
    in_sem, out_sem, fs_send, fs_recv, cs_send, cs_recv, hand_sem,
):
    t = lax.axis_index("tm")
    s = lax.axis_index("space")
    sub, lane = lane_ids()
    masks = {
        "last_sub": sub == SUB - 1, "first_sub": sub == 0,
        "last_lane": lane == LANE - 1, "first_lane": lane == 0,
        "last_cell": (sub == SUB - 1) & (lane == LANE - 1), "first_cell": (sub == 0) & (lane == 0),
        "last_group": lane >= LANE - 4, "first_group": lane < 4,
    }

    def there(dt, ds):
        return (t + dt >= 0) & (t + dt < SLICES) & (s + ds >= 0) & (s + ds < SPACE)

    has_left, has_right = s > 0, s < SPACE - 1

    loads = []
    for k in range(SUB):
        cols = pl.ds(LANE * k, LANE)
        loads.append(pltpu.make_async_copy(lev_ref.at[0, :, :, cols], levb.at[:, :, k, :], in_sem.at[0, k]))
        for d in range(3):
            loads.append(pltpu.make_async_copy(
                vel_ref.at[0, d, :, :, cols], u.at[d, pl.ds(H, ROWS), pl.ds(1, NZ), k, :], in_sem.at[1 + d, k]))
    for c in loads:
        c.start()

    zero_line = jnp.zeros((SUB, LANE), F32)
    cstart[...] = jnp.zeros(cstart.shape, F32)

    barrier = pltpu.get_barrier_semaphore()
    beside = [(0, 1), (0, -1), (1, 0), (-1, 0)]

    def tell(semaphore, places):
        for dt, ds in places:
            @pl.when(there(dt, ds))
            def _(dt=dt, ds=ds):
                pl.semaphore_signal(semaphore, inc=1, device_id=(t + dt, s + ds), device_id_type=MESH)

    def hear(semaphore, places):
        count = jnp.int32(0)
        for dt, ds in places:
            count = count + there(dt, ds).astype(jnp.int32)

        @pl.when(count > 0)
        def _():
            pl.semaphore_wait(semaphore, count)

    tell(barrier, beside)

    def zero_pads(e, _):
        for ref in (c_a, c_b, p1, p_a, p_b, pv.at[1], u.at[0], u.at[1], u.at[2]):
            ref[e, 0] = zero_line
            ref[e, NZ + 1] = zero_line
        return 0

    def zero_rows(first):
        def one(e, _):
            for ref in (c_a, c_b, p1, u.at[0], u.at[1], u.at[2]):
                ref[e] = jnp.zeros((NZ + 2, SUB, LANE), F32)
            return 0
        lax.fori_loop(first, first + H, one, 0)

    def fill_tables():
        lax.fori_loop(0, EXT, zero_pads, 0)

        @pl.when(s == 0)
        def _():
            zero_rows(0)

        @pl.when(s == SPACE - 1)
        def _():
            zero_rows(H + ROWS)

        for ref in (rx1, rx2, rx3, rxs, rxq):
            ref[...] = jnp.zeros(ref.shape, F32)
        strip = sub * 4 + lax.div(lane, TILE)
        tiles = [jnp.clip(lax.div(first_row - 1 + TILE, TILE) - 1, 0, TILES - 1), lax.div(first_row, TILE),
                 jnp.clip(lax.div(first_row + ROWS, TILE), 0, TILES - 1)]
        for f in range(FINE):
            def paint(q, fields, f=f):
                return tuple(jnp.where(strip == q, plan_ref[f, tile, q].astype(F32), field)
                             for tile, field in zip(tiles, fields))
            painted = lax.fori_loop(0, STRIPS, paint, (zero_line,) * 3, unroll=4)
            for j in range(3):
                elec[f, j] = painted[j]
        for z in range(NZ):
            wall[z] = jnp.full((SUB, LANE), wall_scale, F32) * jnp.exp(jnp.full((SUB, LANE), -z / wall_decay, F32))

    first_row = s * ROWS
    for k in range(SUB):
        loads[4 * k].wait()
    for i in range(ROWS):
        c_a[H + i, pl.ds(1, NZ)] = levb[i].astype(F32) * level_scale

    for k in range(SUB):
        for d in range(3):
            loads[4 * k + 1 + d].wait()

    hear(barrier, beside)

    def row_copies(entries, base):
        rights, lefts = [], []
        for n, (ref, skip, count) in enumerate(entries):
            first = H + ROWS - skip - count
            rights.append(pltpu.make_async_remote_copy(
                src_ref=ref.at[pl.ds(first, count), pl.ds(1, NZ)],
                dst_ref=ref.at[pl.ds(first - ROWS, count), pl.ds(1, NZ)],
                send_sem=fs_send.at[base + n, 0], recv_sem=fs_recv.at[base + n, 0],
                device_id=(t, s + 1), device_id_type=MESH))
            first = H + skip
            lefts.append(pltpu.make_async_remote_copy(
                src_ref=ref.at[pl.ds(first, count), pl.ds(1, NZ)],
                dst_ref=ref.at[pl.ds(first + ROWS, count), pl.ds(1, NZ)],
                send_sem=fs_send.at[base + n, 1], recv_sem=fs_recv.at[base + n, 1],
                device_id=(t, s - 1), device_id_type=MESH))
        return rights, lefts

    def start(copies):
        rights, lefts = copies

        @pl.when(has_right)
        def _():
            for c in rights:
                c.start()

        @pl.when(has_left)
        def _():
            for c in lefts:
                c.start()

    def landed(copies):
        rights, lefts = copies

        @pl.when(has_left)
        def _():
            for c in rights:
                c.wait_recv()

        @pl.when(has_right)
        def _():
            for c in lefts:
                c.wait_recv()

    def sent(copies):
        rights, lefts = copies

        @pl.when(has_right)
        def _():
            for c in rights:
                c.wait_send()

        @pl.when(has_left)
        def _():
            for c in lefts:
                c.wait_send()

    def coarse_copy(link, src, ds):
        dst, reach, dt, base, lo, hi = link
        j = reach - ds
        return pltpu.make_async_remote_copy(
            src_ref=src, dst_ref=dst.at[j], send_sem=cs_send.at[base + j], recv_sem=cs_recv.at[base + j],
            device_id=(t + dt, s + ds), device_id_type=MESH)

    def each_target(link, src, action):
        dst, reach, dt, base, lo, hi = link

        @pl.when((t >= lo) & (t <= hi))
        def _():
            def one(j, _):
                ds = j - reach
                ok = there(dt, ds)
                if dt == 0:
                    ok = ok & (ds != 0)

                @pl.when(ok)
                def _():
                    c = coarse_copy(link, src, ds)
                    c.start() if action == "start" else c.wait_send()

                return 0
            lax.fori_loop(0, 2 * reach + 1, one, 0)

    def each_source(link, src):
        dst, reach, dt, base, lo, hi = link

        @pl.when((t - dt >= lo) & (t - dt <= hi))
        def _():
            def one(j, _):
                ds = reach - j
                ok = there(-dt, -ds)
                if dt == 0:
                    ok = ok & (ds != 0)

                @pl.when(ok)
                def _():
                    coarse_copy(link, src, ds).wait_recv()

                return 0
            lax.fori_loop(0, 2 * reach + 1, one, 0)

    starts = (cstart, 2, 0, 0, 0, SLICES - 1)
    one_back = (rx1, 2, 1, 5, 0, SLICES - 2)
    two_back = (rx2, 4, 2, 10, 0, SLICES - 3)
    three_back = (rx3, 6, 3, 19, 0, 0)
    sum_two = (rxs, 4, 2, 32, 2, 5)
    sum_four = (rxq, 8, 4, 41, 2, 3)

    def inside(row):
        return ((row >= 0) & (row < SPACE * ROWS)).astype(F32)

    def over(rows, body):
        lo, hi = rows

        def one(j, _):
            body(lo + lax.div(j, BLOCKS), U * lax.rem(j, BLOCKS))
            return 0
        lax.fori_loop(0, (hi - lo) * BLOCKS, one, 0)

    def six(ref, e, z0):
        mid = ref[e, pl.ds(z0, U + 2)]
        return ref[e - 1, pl.ds(z0 + 1, U)], ref[e + 1, pl.ds(z0 + 1, U)], mid

    def advance(c, new_c, f, e, z0, which, full):
        cxm, cxp, cz = six(c, e, z0)
        uxm, uxp, uz = six(u.at[0], e, z0)
        c0, u0 = cz[1:-1], uz[1:-1]
        cym, cyp = prev_y(c0, masks), next_y(c0, masks)
        w = u[1, e, pl.ds(z0, U + 2)]
        v = u[2, e, pl.ds(z0 + 1, U)]
        vm, vp = prev_y(v, masks), next_y(v, masks)
        net = upwind(c0, cxp, u0, uxp) - upwind(cxm, c0, uxm, u0)
        fz = upwind(cz[:-1], cz[1:], w[:-1], w[1:])
        net = net + (fz[1:] - fz[:-1])
        net = net + (upwind(c0, cyp, v, vp) - upwind(cym, c0, vm, v))
        fresh = c0 - 0.125 * net
        pull = elec[f, which] * wall[pl.ds(z0, U)] / rho_of(c0)
        around = uxm + uxp + uz[:-2] + uz[2:] + prev_y(u0, masks) + next_y(u0, masks)
        px = 0.85 * u0 + (0.025 * around + pull * (cxp - cxm))
        if not full:
            keep = inside(first_row + e - H)
            fresh = fresh * keep
            px = px * keep
        new_c[e, pl.ds(z0 + 1, U)] = fresh
        pv[0, e, pl.ds(z0 + 1, U)] = px
        if full:
            wxm, wxp = u[1, e - 1, pl.ds(z0 + 1, U)], u[1, e + 1, pl.ds(z0 + 1, U)]
            w0_ = w[1:-1]
            around = wxm + wxp + w[:-2] + w[2:] + prev_y(w0_, masks) + next_y(w0_, masks)
            pv[1, e, pl.ds(z0 + 1, U)] = 0.85 * w0_ + (0.025 * around + pull * (cz[2:] - cz[:-2]))
            vxm, vxp, vz = six(u.at[2], e, z0)
            around = vxm + vxp + vz[:-2] + vz[2:] + vm + vp
            pv[2, e, pl.ds(z0 + 1, U)] = 0.85 * v + (0.025 * around + pull * (cyp - cym))

    def face_block(new_c, e, z0, top):
        rz = rho_of(new_c[e, pl.ds(z0, U + 2)])
        r0 = rz[1:-1]
        rxm = rho_of(new_c[e - 1, pl.ds(z0 + 1, U)])
        rxp = rho_of(new_c[e + 1, pl.ds(z0 + 1, U)])
        lower = 1.0 / (rxm + r0)
        upper = 1.0 / (rxp + r0)
        gx[e, pl.ds(z0, U)] = lower
        gx[e + 1, pl.ds(z0, U)] = upper
        zface = 1.0 / (rz[:-1] + rz[1:])
        gz[e, pl.ds(z0, U + 1)] = zface
        yl = 1.0 / (r0 + prev_y(r0, masks, 0.1))
        yu = 1.0 / (r0 + next_y(r0, masks, 0.1))
        gyl[e, pl.ds(z0, U)] = jnp.where(masks["first_cell"], 0.0, yl)
        gyu[e, pl.ds(z0, U)] = jnp.where(masks["last_cell"], 0.0, yu)
        total = lower + upper + (zface[:-1] + zface[1:]) + (yl + yu)
        inverse = 1.0 / total
        if not top:
            inverse = inverse * inside(first_row + e - H)
        rt[e, pl.ds(z0, U)] = inverse
        return inverse

    def first_pressure(new_c, e, z0):
        inverse = face_block(new_c, e, z0, True)
        pz = pv[1, e, pl.ds(z0, U + 2)]
        py = pv[2, e, pl.ds(z0 + 1, U)]
        source = pv[0, e + 1, pl.ds(z0 + 1, U)] - pv[0, e - 1, pl.ds(z0 + 1, U)]
        source = source + (pz[2:] - pz[:-2]) + (next_y(py, masks) - prev_y(py, masks))
        p1[e, pl.ds(z0 + 1, U)] = -(source * inverse)

    def sweep(old, new, e, z0):
        pxm, pxp, pz = six(old, e, z0)
        p0 = pz[1:-1]
        zface = gz[e, pl.ds(z0, U + 1)]
        summed = gx[e, pl.ds(z0, U)] * pxm + gx[e + 1, pl.ds(z0, U)] * pxp
        summed = summed + (zface[:-1] * pz[:-2] + zface[1:] * pz[2:])
        summed = summed + (gyl[e, pl.ds(z0, U)] * prev_y(p0, masks, None) + gyu[e, pl.ds(z0, U)] * next_y(p0, masks, None))
        new[e, pl.ds(z0 + 1, U)] = p1[e, pl.ds(z0 + 1, U)] + rt[e, pl.ds(z0, U)] * summed

    def project(new_c, e, z0):
        pxm, pxp, pz = six(p_a, e, z0)
        p0 = pz[1:-1]
        scale = 0.125 / rho_of(new_c[e, pl.ds(z0 + 1, U)])
        zs = pl.ds(z0 + 1, U)
        u[0, e, zs] = pv[0, e, zs] - scale * (pxp - pxm)
        u[1, e, zs] = pv[1, e, zs] - scale * (pz[2:] - pz[:-2])
        u[2, e, zs] = pv[2, e, zs] - scale * (next_y(p0, masks) - prev_y(p0, masks))

    even, low = lax.rem(lane, 2) == 0, lax.rem(lane, 4) < 2
    spread = jnp.where(lax.rem(lane, 4) == 0, fraction_spread, velocity_spread).astype(F32)

    def combine(a, b, by, mask):
        keep, other = jnp.where(mask, a, b), jnp.where(mask, b, a)
        return keep + jnp.where(mask, roll(other, LANE - by, 2), roll(other, by, 2))

    def restrict(c, out):
        sums = []
        for ref in (c, u.at[0], u.at[1], u.at[2]):
            total = None
            for i in range(ROWS):
                part = ref[H + i, pl.ds(1, NZ)]
                total = part if total is None else total + part
            sums.append(jnp.sum(total.reshape(4, 4, SUB, LANE), axis=1))
        pair = combine(sums[0], sums[1], 1, even), combine(sums[2], sums[3], 1, even)
        out[...] = combine(pair[0], pair[1], 2, low) * (1.0 / 64.0)

    def diffuse(src, dst, length, out_reach):
        whole = src[pl.ds(0, length + 2)]
        v = whole[1:-1]
        edge = jnp.zeros((length, 1, SUB, LANE), F32)
        up = jnp.concatenate([v[:, 1:], edge], axis=1)
        down = jnp.concatenate([edge, v[:, :-1]], axis=1)
        around = whole[:-2] + whole[2:] + up + down + next_y(v, masks, by=4) + prev_y(v, masks, by=4)
        fresh = v + spread * (around - 6.0 * v)
        for j in range(length):
            row = s + j - out_reach
            keep = ((row >= 0) & (row < SPACE)).astype(F32)
            dst[j] = fresh[j] * keep

    def diffuse_down(src, reach, steps):
        now = src
        for step in range(steps):
            reach -= 1
            target = w0 if step % 2 == 0 else w1
            diffuse(now, target, 2 * reach + 1, reach)
            now = target
        return now

    near = row_copies([(c_a, 0, 1), (u.at[0], 0, 1), (u.at[1], 0, 1), (u.at[2], 0, 1)], 0)
    far = row_copies([(c_a, 1, 1), (u.at[0], 1, 1)], 4)
    start(near)
    start(far)
    tell(hand_sem.at[0], [(1, 0), (-1, 0)])
    fill_tables()
    restrict(c_a, cstart.at[2])

    def both(body, *rows):
        for e in rows:
            body(e, 0)

    c, new_c = c_a, c_b
    last = H + ROWS - 1
    for f in range(FINE):
        def step_full(e, z0):
            advance(c, new_c, f, e, z0, 1, True)

        def faces(e, z0):
            face_block(new_c, e, z0, False)

        def first_p(e, z0):
            first_pressure(new_c, e, z0)

        def sweep_1(e, z0):
            sweep(p1, p_a, e, z0)

        def sweep_2(e, z0):
            sweep(p_a, p_b, e, z0)

        def sweep_3(e, z0):
            sweep(p_b, p_a, e, z0)

        base = 6 + 10 * f
        over((H + 1, last), step_full)
        fraction_mid = row_copies([(new_c, 1, 2)], base)
        start(fraction_mid)
        landed(near)
        both(step_full, H, last)
        fraction_far = row_copies([(new_c, 3, 1)], base + 1)
        start(fraction_far)
        over((H + 1, last), first_p)
        pressure_mid = row_copies([(p1, 1, 2)], base + 2)
        start(pressure_mid)
        if f == 0:
            hear(hand_sem.at[0], [(1, 0), (-1, 0)])
            tell(hand_sem.at[1], [(2, 0), (-2, 0)])
            each_target(starts, cstart.at[2], "start")
        else:
            hear(hand_sem.at[1], [(2, 0), (-2, 0)])
            tell(hand_sem.at[2], [(0, 4), (0, -4)])
        landed(far)
        advance(c, new_c, f, H - 1, 0, 0, False)
        advance(c, new_c, f, last + 1, 0, 2, False)
        both(first_p, H, last)
        pressure_near = row_copies([(p1, 0, 1)], base + 3)
        pressure_far = row_copies([(p1, 3, 1)], base + 4)
        start(pressure_near)
        start(pressure_far)
        over((H + 1, last), sweep_1)
        landed(fraction_mid)
        both(faces, H - 1, last + 1)
        landed(fraction_far)
        both(faces, H - 2, last + 2)
        both(faces, H - 3, last + 3)
        if f == 0:
            each_source(starts, cstart.at[2])
            done = diffuse_down(cstart, 2, 2)
            prev[...] = done[0] * (t > 0).astype(F32)
        else:
            hear(hand_sem.at[2], [(0, 4), (0, -4)])
            tell(hand_sem.at[3], [(-k, 0) for k in (1, 2, 3, 4)])
        landed(pressure_mid)
        landed(pressure_near)
        both(sweep_1, H, last)
        both(sweep_1, H - 1, last + 1)
        both(sweep_1, H - 2, last + 2)
        over((H - 1, last + 2), sweep_2)
        over((H, last + 1), sweep_3)
        landed(pressure_far)
        both(sweep_1, H - 3, last + 3)
        both(sweep_2, H - 2, last + 2)
        both(sweep_3, H - 1, last + 1)
        sent(near)
        sent(far)
        over((H, H + ROWS), lambda e, z0: project(new_c, e, z0))
        if f == 0:
            near = row_copies([(u.at[0], 0, 1), (u.at[1], 0, 1), (u.at[2], 0, 1)], 26)
            far = row_copies([(u.at[0], 1, 1)], 29)
            start(near)
            start(far)
        for copies in (fraction_mid, fraction_far, pressure_mid, pressure_near, pressure_far):
            sent(copies)
        c, new_c = new_c, c
    each_target(starts, cstart.at[2], "sent")

    restrict(c, drive)
    drive[...] = drive[...] - prev[...]
    hear(hand_sem.at[3], [(k, 0) for k in (1, 2, 3, 4)])
    each_target(three_back, drive, "start")
    each_target(two_back, drive, "start")
    each_target(one_back, drive, "start")
    each_source(three_back, drive)
    three = diffuse_down(rx3, 6, 2)
    each_source(two_back, drive)
    three[pl.ds(0, 9)] = three[pl.ds(0, 9)] + rx2[...]
    diffuse(three, w0, 7, 3)
    diffuse(w0, w1, 5, 2)
    each_source(one_back, drive)
    w1[pl.ds(0, 5)] = w1[pl.ds(0, 5)] + rx1[...]
    diffuse(w1, w0, 3, 1)
    diffuse(w0, w1, 1, 0)
    part[...] = w1[0]
    each_target(sum_four, part, "start")
    each_target(sum_two, part, "start")
    each_source(sum_four, part)
    eight = diffuse_down(rxq, 8, 4)
    each_source(sum_two, part)
    eight[pl.ds(0, 9)] = eight[pl.ds(0, 9)] + rxs[...]
    four = diffuse_down(eight, 4, 4)
    correction = (part[...] + four[0]) - prev[...]

    stores = []
    for field in range(4):
        target = c if field == 0 else u.at[field - 1]

        m = jnp.where(lax.rem(lane, 4) == field, correction, 0.0)
        m = m + roll(m, 1 if field % 2 == 0 else LANE - 1, 2)
        m = m + roll(m, 2 if field < 2 else LANE - 2, 2)
        m = jnp.broadcast_to(m[:, None], (4, 4, SUB, LANE)).reshape(NZ, SUB, LANE)
        for i in range(ROWS):
            target[H + i, pl.ds(1, NZ)] = target[H + i, pl.ds(1, NZ)] + m
        for k in range(SUB):
            cols = pl.ds(LANE * k, LANE)
            home = ofrac_ref.at[0, :, :, cols] if field == 0 else ovel_ref.at[0, field - 1, :, :, cols]
            stores.append(pltpu.make_async_copy(
                target.at[pl.ds(H, ROWS), pl.ds(1, NZ), k, :], home, out_sem.at[field, k]))
            stores[-1].start()
    each_target(three_back, drive, "sent")
    each_target(two_back, drive, "sent")
    each_target(one_back, drive, "sent")
    each_target(sum_four, part, "sent")
    each_target(sum_two, part, "sent")
    for c_ in stores:
        c_.wait()


def shards(fraction_levels, start_velocity, electrode_plan):
    line = (SUB, LANE)
    pad = (EXT, NZ + 2) + line
    flat = (EXT, NZ) + line
    row = (4,) + line

    def vmem(*shape):
        return pltpu.VMEM(shape, F32)

    return pl.pallas_call(
        kernel,
        out_shape=(
            jax.ShapeDtypeStruct(fraction_levels.shape, F32),
            jax.ShapeDtypeStruct(start_velocity.shape, F32),
        ),
        in_specs=[
            pl.BlockSpec(memory_space=pl.ANY),
            pl.BlockSpec(memory_space=pl.ANY),
            pl.BlockSpec(memory_space=pltpu.SMEM),
        ],
        out_specs=(pl.BlockSpec(memory_space=pl.ANY), pl.BlockSpec(memory_space=pl.ANY)),
        scratch_shapes=[
            pltpu.VMEM((ROWS, NZ) + line, jnp.int32),
            vmem(*pad), vmem(*pad),
            vmem(3, *pad), vmem(3, *pad),
            vmem(EXT + 1, NZ, *line), vmem(*pad), vmem(*flat), vmem(*flat), vmem(*flat),
            vmem(*pad), vmem(*pad), vmem(*pad),
            vmem(FINE, 3, *line), vmem(NZ, *line),
            vmem(5, *row), vmem(*row), vmem(*row),
            vmem(5, *row), vmem(9, *row), vmem(13, *row), vmem(9, *row), vmem(17, *row),
            vmem(*row), vmem(17, *row), vmem(17, *row),
            pltpu.SemaphoreType.DMA((4, SUB)), pltpu.SemaphoreType.DMA((4, SUB)),
            pltpu.SemaphoreType.DMA((30, 2)), pltpu.SemaphoreType.DMA((30, 2)),
            pltpu.SemaphoreType.DMA((58,)), pltpu.SemaphoreType.DMA((58,)),
            pltpu.SemaphoreType.REGULAR((4,)),
        ],
        compiler_params=pltpu.CompilerParams(
            collective_id=0, has_side_effects=True, vmem_limit_bytes=62 * 2**20
        ),
    )(fraction_levels, start_velocity, electrode_plan)


def solution(mesh):
    return jax.shard_map(
        shards,
        mesh=mesh,
        in_specs=(
            P("tm", "space", None, None),
            P("tm", None, "space", None, None),
            P("tm", None, None),
        ),
        out_specs=(P("tm", "space", None, None), P("tm", None, "space", None, None)),
        check_vma=False,
    )
```

```python
import functools

import jax
import jax.numpy as jnp
from jax import lax
from jax.experimental import pallas as pl
from jax.experimental.pallas import tpu as pltpu
from jax.sharding import PartitionSpec as P

MESH = pl.DeviceIdType.MESH
F32 = jnp.float32

ROWS = 4
NZ = 16
SUB, LANE = 8, 128
H = 4
EXT = ROWS + 2 * H
TILE = 32
TILES = 4
STRIPS = 32
FINE = 2
U = 16
BLOCKS = NZ // U

SLICES, SPACE = 8, 32
wall_scale = 1.5 * 0.25 * 0.5
wall_decay = 4.0
level_scale = 1.0 / 1024.0
fraction_spread, velocity_spread = 0.05, 0.15


def lane_ids():
    sub = lax.broadcasted_iota(jnp.int32, (SUB, LANE), 0)
    lane = lax.broadcasted_iota(jnp.int32, (SUB, LANE), 1)
    return sub, lane


def roll(v, by, axis):
    return pltpu.roll(v, by, axis)


def next_y(v, masks, fill=0.0, by=1):
    ax = v.ndim
    r = roll(v, LANE - by, ax - 1)
    q = roll(r, SUB - 1, ax - 2)
    if fill is not None:
        q = jnp.where(masks["last_sub"], fill, q)
    return jnp.where(masks["last_lane"] if by == 1 else masks["last_group"], q, r)


def prev_y(v, masks, fill=0.0, by=1):
    ax = v.ndim
    r = roll(v, by, ax - 1)
    q = roll(r, 1, ax - 2)
    if fill is not None:
        q = jnp.where(masks["first_sub"], fill, q)
    return jnp.where(masks["first_lane"] if by == 1 else masks["first_group"], q, r)


def upwind(lower, upper, speed_lower, speed_upper):
    speed = speed_lower + speed_upper
    return speed * jnp.where(speed > 0.0, lower, upper)


def rho_of(c):
    return 0.1 + 0.9 * jnp.clip(c, 0.0, 1.0)


def kernel(
    lev_ref, vel_ref, plan_ref, ofrac_ref, ovel_ref, cfrac_ref, cvel_ref,
    levb, c_a, c_b, u, pv, gx, gz, gyl, gyu, rt, p1, p_a, p_b, elec, wall,
    cstart, prev, drive, rx1, rx2, rx3, rxs, rxq, part, w0, w1, wide,
    in_sem, out_sem, fs_send, fs_recv, cs_send, cs_recv, hand_sem,
):
    t = lax.axis_index("tm")
    s = lax.axis_index("space")
    sub, lane = lane_ids()
    masks = {
        "last_sub": sub == SUB - 1, "first_sub": sub == 0,
        "last_lane": lane == LANE - 1, "first_lane": lane == 0,
        "last_cell": (sub == SUB - 1) & (lane == LANE - 1), "first_cell": (sub == 0) & (lane == 0),
        "last_group": lane >= LANE - 4, "first_group": lane < 4,
    }

    def there(dt, ds):
        return (t + dt >= 0) & (t + dt < SLICES) & (s + ds >= 0) & (s + ds < SPACE)

    has_left, has_right = s > 0, s < SPACE - 1

    loads = {}
    for i in (0, ROWS - 1, 1, 2):
        loads[i] = []
        for k in range(SUB):
            cols = pl.ds(LANE * k, LANE)
            loads[i].append(pltpu.make_async_copy(
                lev_ref.at[0, i, :, cols], levb.at[i, :, k, :], in_sem.at[0, i, k]))
            loads[i].append(pltpu.make_async_copy(
                vel_ref.at[0, :, i, :, cols], u.at[:, H + i, pl.ds(1, NZ), k, :], in_sem.at[1, i, k]))
        for n, c in enumerate(loads[i]):
            c.start(priority=n // 2 % 2)

    zero_line = jnp.zeros((SUB, LANE), F32)
    cstart[...] = jnp.zeros(cstart.shape, F32)

    barrier = pltpu.get_barrier_semaphore()
    beside = [(0, 1), (0, -1), (1, 0), (-1, 0)]

    def tell(semaphore, places):
        for dt, ds in places:
            @pl.when(there(dt, ds))
            def _(dt=dt, ds=ds):
                pl.semaphore_signal(semaphore, inc=1, device_id=(t + dt, s + ds), device_id_type=MESH)

    def hear(semaphore, places):
        count = jnp.int32(0)
        for dt, ds in places:
            count = count + there(dt, ds).astype(jnp.int32)

        @pl.when(count > 0)
        def _():
            pl.semaphore_wait(semaphore, count)

    tell(barrier, beside)

    def zero_pads(e, _):
        for ref in (c_a, c_b, p1, p_a, p_b, pv.at[1], u.at[0], u.at[1], u.at[2]):
            ref[e, 0] = zero_line
            ref[e, NZ + 1] = zero_line
        return 0

    def zero_rows(first):
        def one(e, _):
            for ref in (c_a, c_b, p1, u.at[0], u.at[1], u.at[2]):
                ref[e] = jnp.zeros((NZ + 2, SUB, LANE), F32)
            return 0
        lax.fori_loop(first, first + H, one, 0)

    def fill_tables():
        lax.fori_loop(0, EXT, zero_pads, 0)

        @pl.when(s == 0)
        def _():
            zero_rows(0)

        @pl.when(s == SPACE - 1)
        def _():
            zero_rows(H + ROWS)

        for ref in (rx1, rx2, rx3, rxs, rxq):
            ref[...] = jnp.zeros(ref.shape, F32)
        strip = sub * 4 + lax.div(lane, TILE)
        tiles = [jnp.clip(lax.div(first_row - 1 + TILE, TILE) - 1, 0, TILES - 1), lax.div(first_row, TILE),
                 jnp.clip(lax.div(first_row + ROWS, TILE), 0, TILES - 1)]
        for f in range(FINE):
            def paint(q, fields, f=f):
                return tuple(jnp.where(strip == q, plan_ref[f, tile, q].astype(F32), field)
                             for tile, field in zip(tiles, fields))
            painted = lax.fori_loop(0, STRIPS, paint, (zero_line,) * 3, unroll=4)
            for j in range(3):
                elec[f, j] = painted[j]
        for z in range(NZ):
            wall[z] = jnp.full((SUB, LANE), wall_scale, F32) * jnp.exp(jnp.full((SUB, LANE), -z / wall_decay, F32))

    first_row = s * ROWS
    def load(i):
        for c in loads[i]:
            c.wait()
        c_a[H + i, pl.ds(1, NZ)] = levb[i].astype(F32) * level_scale

    load(0)
    load(ROWS - 1)
    hear(barrier, beside)

    def row_copies(entries, base):
        rights, lefts = [], []
        for n, (ref, skip, count) in enumerate(entries):
            first = H + ROWS - skip - count
            rights.append(pltpu.make_async_remote_copy(
                src_ref=ref.at[pl.ds(first, count), pl.ds(1, NZ)],
                dst_ref=ref.at[pl.ds(first - ROWS, count), pl.ds(1, NZ)],
                send_sem=fs_send.at[base + n, 0], recv_sem=fs_recv.at[base + n, 0],
                device_id=(t, s + 1), device_id_type=MESH))
            first = H + skip
            lefts.append(pltpu.make_async_remote_copy(
                src_ref=ref.at[pl.ds(first, count), pl.ds(1, NZ)],
                dst_ref=ref.at[pl.ds(first + ROWS, count), pl.ds(1, NZ)],
                send_sem=fs_send.at[base + n, 1], recv_sem=fs_recv.at[base + n, 1],
                device_id=(t, s - 1), device_id_type=MESH))
        return rights, lefts

    def start(copies):
        rights, lefts = copies

        @pl.when(has_right)
        def _():
            for c in rights:
                c.start()

        @pl.when(has_left)
        def _():
            for c in lefts:
                c.start()

    def landed(copies):
        rights, lefts = copies

        @pl.when(has_left)
        def _():
            for c in rights:
                c.wait_recv()

        @pl.when(has_right)
        def _():
            for c in lefts:
                c.wait_recv()

    def sent(copies):
        rights, lefts = copies

        @pl.when(has_right)
        def _():
            for c in rights:
                c.wait_send()

        @pl.when(has_left)
        def _():
            for c in lefts:
                c.wait_send()

    def coarse_copy(link, src, ds):
        dst, reach, dt, base, lo, hi = link
        j = reach - ds
        return pltpu.make_async_remote_copy(
            src_ref=src, dst_ref=dst.at[j], send_sem=cs_send.at[base + j], recv_sem=cs_recv.at[base + j],
            device_id=(t + dt, s + ds), device_id_type=MESH)

    def each_target(link, src, action):
        dst, reach, dt, base, lo, hi = link

        @pl.when((t >= lo) & (t <= hi))
        def _():
            def one(j, _):
                ds = j - reach
                ok = there(dt, ds)
                if dt == 0:
                    ok = ok & (ds != 0)

                @pl.when(ok)
                def _():
                    c = coarse_copy(link, src, ds)
                    c.start() if action == "start" else c.wait_send()

                return 0
            lax.fori_loop(0, 2 * reach + 1, one, 0)

    def each_source(link, src):
        dst, reach, dt, base, lo, hi = link

        @pl.when((t - dt >= lo) & (t - dt <= hi))
        def _():
            def one(j, _):
                ds = reach - j
                ok = there(-dt, -ds)
                if dt == 0:
                    ok = ok & (ds != 0)

                @pl.when(ok)
                def _():
                    coarse_copy(link, src, ds).wait_recv()

                return 0
            lax.fori_loop(0, 2 * reach + 1, one, 0)

    starts = (cstart, 2, 0, 0, 0, SLICES - 1)
    one_back = (rx1, 2, 1, 5, 0, SLICES - 2)
    two_back = (rx2, 4, 2, 10, 0, SLICES - 3)
    three_back = (rx3, 6, 3, 19, 0, 0)
    sum_two = (rxs, 4, 2, 32, 2, 5)
    sum_four = (rxq, 8, 4, 41, 2, 3)

    def inside(row):
        return ((row >= 0) & (row < SPACE * ROWS)).astype(F32)

    def over(rows, body):
        lo, hi = rows

        def one(j, _):
            body(lo + lax.div(j, BLOCKS), U * lax.rem(j, BLOCKS))
            return 0
        lax.fori_loop(0, (hi - lo) * BLOCKS, one, 0)

    def six(ref, e, z0):
        mid = ref[e, pl.ds(z0, U + 2)]
        return ref[e - 1, pl.ds(z0 + 1, U)], ref[e + 1, pl.ds(z0 + 1, U)], mid

    def advance(c, new_c, f, e, z0, which, full):
        cxm, cxp, cz = six(c, e, z0)
        uxm, uxp, uz = six(u.at[0], e, z0)
        c0, u0 = cz[1:-1], uz[1:-1]
        cym, cyp = prev_y(c0, masks), next_y(c0, masks)
        w = u[1, e, pl.ds(z0, U + 2)]
        v = u[2, e, pl.ds(z0 + 1, U)]
        vm, vp = prev_y(v, masks), next_y(v, masks)
        net = upwind(c0, cxp, u0, uxp) - upwind(cxm, c0, uxm, u0)
        fz = upwind(cz[:-1], cz[1:], w[:-1], w[1:])
        net = net + (fz[1:] - fz[:-1])
        net = net + (upwind(c0, cyp, v, vp) - upwind(cym, c0, vm, v))
        fresh = c0 - 0.125 * net
        pull = elec[f, which] * wall[pl.ds(z0, U)] / rho_of(c0)
        around = uxm + uxp + uz[:-2] + uz[2:] + prev_y(u0, masks) + next_y(u0, masks)
        px = 0.85 * u0 + (0.025 * around + pull * (cxp - cxm))
        if not full:
            keep = inside(first_row + e - H)
            fresh = fresh * keep
            px = px * keep
        new_c[e, pl.ds(z0 + 1, U)] = fresh
        pv[0, e, pl.ds(z0 + 1, U)] = px
        if full:
            wxm, wxp = u[1, e - 1, pl.ds(z0 + 1, U)], u[1, e + 1, pl.ds(z0 + 1, U)]
            w0_ = w[1:-1]
            around = wxm + wxp + w[:-2] + w[2:] + prev_y(w0_, masks) + next_y(w0_, masks)
            pv[1, e, pl.ds(z0 + 1, U)] = 0.85 * w0_ + (0.025 * around + pull * (cz[2:] - cz[:-2]))
            vxm, vxp, vz = six(u.at[2], e, z0)
            around = vxm + vxp + vz[:-2] + vz[2:] + vm + vp
            pv[2, e, pl.ds(z0 + 1, U)] = 0.85 * v + (0.025 * around + pull * (cyp - cym))

    def face_block(new_c, e, z0, top):
        rz = rho_of(new_c[e, pl.ds(z0, U + 2)])
        r0 = rz[1:-1]
        rxm = rho_of(new_c[e - 1, pl.ds(z0 + 1, U)])
        rxp = rho_of(new_c[e + 1, pl.ds(z0 + 1, U)])
        lower = 1.0 / (rxm + r0)
        upper = 1.0 / (rxp + r0)
        gx[e, pl.ds(z0, U)] = lower
        gx[e + 1, pl.ds(z0, U)] = upper
        zface = 1.0 / (rz[:-1] + rz[1:])
        gz[e, pl.ds(z0, U + 1)] = zface
        yl = 1.0 / (r0 + prev_y(r0, masks, 0.1))
        yu = 1.0 / (r0 + next_y(r0, masks, 0.1))
        gyl[e, pl.ds(z0, U)] = jnp.where(masks["first_cell"], 0.0, yl)
        gyu[e, pl.ds(z0, U)] = jnp.where(masks["last_cell"], 0.0, yu)
        total = lower + upper + (zface[:-1] + zface[1:]) + (yl + yu)
        inverse = 1.0 / total
        if not top:
            inverse = inverse * inside(first_row + e - H)
        rt[e, pl.ds(z0, U)] = inverse
        return inverse

    def first_pressure(new_c, e, z0):
        inverse = face_block(new_c, e, z0, True)
        pz = pv[1, e, pl.ds(z0, U + 2)]
        py = pv[2, e, pl.ds(z0 + 1, U)]
        source = pv[0, e + 1, pl.ds(z0 + 1, U)] - pv[0, e - 1, pl.ds(z0 + 1, U)]
        source = source + (pz[2:] - pz[:-2]) + (next_y(py, masks) - prev_y(py, masks))
        p1[e, pl.ds(z0 + 1, U)] = -(source * inverse)

    def sweep(old, new, e, z0):
        pxm, pxp, pz = six(old, e, z0)
        p0 = pz[1:-1]
        zface = gz[e, pl.ds(z0, U + 1)]
        summed = gx[e, pl.ds(z0, U)] * pxm + gx[e + 1, pl.ds(z0, U)] * pxp
        summed = summed + (zface[:-1] * pz[:-2] + zface[1:] * pz[2:])
        summed = summed + (gyl[e, pl.ds(z0, U)] * prev_y(p0, masks, None) + gyu[e, pl.ds(z0, U)] * next_y(p0, masks, None))
        new[e, pl.ds(z0 + 1, U)] = p1[e, pl.ds(z0 + 1, U)] + rt[e, pl.ds(z0, U)] * summed

    def project(new_c, e, z0):
        pxm, pxp, pz = six(p_a, e, z0)
        p0 = pz[1:-1]
        scale = 0.125 / rho_of(new_c[e, pl.ds(z0 + 1, U)])
        zs = pl.ds(z0 + 1, U)
        u[0, e, zs] = pv[0, e, zs] - scale * (pxp - pxm)
        u[1, e, zs] = pv[1, e, zs] - scale * (pz[2:] - pz[:-2])
        u[2, e, zs] = pv[2, e, zs] - scale * (next_y(p0, masks) - prev_y(p0, masks))

    even, low = lax.rem(lane, 2) == 0, lax.rem(lane, 4) < 2
    spread = jnp.where(lax.rem(lane, 4) == 0, fraction_spread, velocity_spread).astype(F32)

    def combine(a, b, by, mask):
        keep, other = jnp.where(mask, a, b), jnp.where(mask, b, a)
        return keep + jnp.where(mask, roll(other, LANE - by, 2), roll(other, by, 2))

    def restrict(c, out):
        sums = []
        for ref in (c, u.at[0], u.at[1], u.at[2]):
            total = None
            for i in range(ROWS):
                part = ref[H + i, pl.ds(1, NZ)]
                total = part if total is None else total + part
            sums.append(jnp.sum(total.reshape(4, 4, SUB, LANE), axis=1))
        pair = combine(sums[0], sums[1], 1, even), combine(sums[2], sums[3], 1, even)
        out[...] = combine(pair[0], pair[1], 2, low) * (1.0 / 64.0)

    def diffuse(src, dst, length, out_reach):
        whole = src[pl.ds(0, length + 2)]
        v = whole[1:-1]
        edge = jnp.zeros((length, 1, SUB, LANE), F32)
        up = jnp.concatenate([v[:, 1:], edge], axis=1)
        down = jnp.concatenate([edge, v[:, :-1]], axis=1)
        around = whole[:-2] + whole[2:] + up + down + next_y(v, masks, by=4) + prev_y(v, masks, by=4)
        fresh = v + spread * (around - 6.0 * v)
        for j in range(length):
            row = s + j - out_reach
            keep = ((row >= 0) & (row < SPACE)).astype(F32)
            dst[j] = fresh[j] * keep

    def diffuse_down(src, reach, steps):
        now = src
        for step in range(steps):
            reach -= 1
            target = w0 if step % 2 == 0 else w1
            diffuse(now, target, 2 * reach + 1, reach)
            now = target
        return now

    near = row_copies([(c_a, 0, 1), (u.at[0], 0, 1), (u.at[1], 0, 1), (u.at[2], 0, 1)], 0)
    far = row_copies([(c_a, 1, 1), (u.at[0], 1, 1)], 4)
    start(near)
    load(1)
    load(2)
    start(far)
    tell(hand_sem.at[0], [(1, 0), (-1, 0)])
    fill_tables()
    restrict(c_a, cstart.at[2])

    def both(body, *rows):
        for e in rows:
            body(e, 0)

    c, new_c = c_a, c_b
    last = H + ROWS - 1
    for f in range(FINE):
        def step_full(e, z0):
            advance(c, new_c, f, e, z0, 1, True)

        def faces(e, z0):
            face_block(new_c, e, z0, False)

        def first_p(e, z0):
            first_pressure(new_c, e, z0)

        def sweep_1(e, z0):
            sweep(p1, p_a, e, z0)

        def sweep_2(e, z0):
            sweep(p_a, p_b, e, z0)

        def sweep_3(e, z0):
            sweep(p_b, p_a, e, z0)

        base = 6 + 10 * f
        over((H + 1, last), step_full)
        fraction_mid = row_copies([(new_c, 1, 2)], base)
        start(fraction_mid)
        landed(near)
        both(step_full, H, last)
        fraction_far = row_copies([(new_c, 3, 1)], base + 1)
        start(fraction_far)
        over((H + 1, last), first_p)
        pressure_mid = row_copies([(p1, 1, 2)], base + 2)
        start(pressure_mid)
        if f == 0:
            hear(hand_sem.at[0], [(1, 0), (-1, 0)])
            tell(hand_sem.at[1], [(2, 0), (-2, 0)])
            each_target(starts, cstart.at[2], "start")
        else:
            hear(hand_sem.at[1], [(2, 0), (-2, 0)])
            tell(hand_sem.at[2], [(0, 4), (0, -4)])
        landed(far)
        advance(c, new_c, f, H - 1, 0, 0, False)
        advance(c, new_c, f, last + 1, 0, 2, False)
        both(first_p, H, last)
        pressure_near = row_copies([(p1, 0, 1)], base + 3)
        pressure_far = row_copies([(p1, 3, 1)], base + 4)
        start(pressure_near)
        start(pressure_far)
        over((H + 1, last), sweep_1)
        landed(fraction_mid)
        both(faces, H - 1, last + 1)
        landed(fraction_far)
        both(faces, H - 2, last + 2)
        both(faces, H - 3, last + 3)
        if f == 0:
            each_source(starts, cstart.at[2])
            done = diffuse_down(cstart, 2, 2)
            prev[...] = done[0] * (t > 0).astype(F32)
        else:
            hear(hand_sem.at[2], [(0, 4), (0, -4)])
            tell(hand_sem.at[3], [(-k, 0) for k in (1, 2, 3, 4)])
        landed(pressure_mid)
        landed(pressure_near)
        both(sweep_1, H, last)
        both(sweep_1, H - 1, last + 1)
        both(sweep_1, H - 2, last + 2)
        over((H - 1, last + 2), sweep_2)
        over((H, last + 1), sweep_3)
        landed(pressure_far)
        both(sweep_1, H - 3, last + 3)
        both(sweep_2, H - 2, last + 2)
        both(sweep_3, H - 1, last + 1)
        sent(near)
        sent(far)
        over((H, H + ROWS), lambda e, z0: project(new_c, e, z0))
        if f == 0:
            near = row_copies([(u.at[0], 0, 1), (u.at[1], 0, 1), (u.at[2], 0, 1)], 26)
            far = row_copies([(u.at[0], 1, 1)], 29)
            start(near)
            start(far)
        for copies in (fraction_mid, fraction_far, pressure_mid, pressure_near, pressure_far):
            sent(copies)
        c, new_c = new_c, c
    each_target(starts, cstart.at[2], "sent")

    stores = []
    for k in range(SUB):
        cols = pl.ds(LANE * k, LANE)
        stores.append(pltpu.make_async_copy(
            c.at[pl.ds(H, ROWS), pl.ds(1, NZ), k, :], ofrac_ref.at[0, :, :, cols], out_sem.at[0, k]))
        stores.append(pltpu.make_async_copy(
            u.at[:, pl.ds(H, ROWS), pl.ds(1, NZ), k, :], ovel_ref.at[0, :, :, :, cols], out_sem.at[1, k]))
    restrict(c, drive)
    drive[...] = drive[...] - prev[...]
    hear(hand_sem.at[3], [(k, 0) for k in (1, 2, 3, 4)])
    each_target(three_back, drive, "start")
    each_target(two_back, drive, "start")
    each_target(one_back, drive, "start")
    for c_ in stores:
        c_.start()
    each_source(three_back, drive)
    three = diffuse_down(rx3, 6, 2)
    each_source(two_back, drive)
    three[pl.ds(0, 9)] = three[pl.ds(0, 9)] + rx2[...]
    diffuse(three, w0, 7, 3)
    diffuse(w0, w1, 5, 2)
    each_source(one_back, drive)
    w1[pl.ds(0, 5)] = w1[pl.ds(0, 5)] + rx1[...]
    diffuse(w1, w0, 3, 1)
    diffuse(w0, w1, 1, 0)
    part[...] = w1[0]
    each_target(sum_four, part, "start")
    each_target(sum_two, part, "start")
    each_source(sum_four, part)
    eight = diffuse_down(rxq, 8, 4)
    each_source(sum_two, part)
    eight[pl.ds(0, 9)] = eight[pl.ds(0, 9)] + rxs[...]
    four = diffuse_down(eight, 4, 4)
    correction = (part[...] + four[0]) - prev[...]

    for field in range(4):
        m = jnp.where(lax.rem(lane, 4) == field, correction, 0.0)
        m = m + roll(m, 1 if field % 2 == 0 else LANE - 1, 2)
        m = m + roll(m, 2 if field < 2 else LANE - 2, 2)
        wide[field] = jnp.broadcast_to(m[:, None], (4, 4, SUB, LANE)).reshape(NZ, SUB, LANE)
    for k in range(SUB):
        cols = pl.ds(LANE * k, LANE)
        stores.append(pltpu.make_async_copy(wide.at[0, :, k, :], cfrac_ref.at[:, cols], out_sem.at[2, k]))
        stores.append(pltpu.make_async_copy(wide.at[1:4, :, k, :], cvel_ref.at[:, :, cols], out_sem.at[3, k]))
        stores[-2].start()
        stores[-1].start(priority=1)
    each_target(three_back, drive, "sent")
    each_target(two_back, drive, "sent")
    each_target(one_back, drive, "sent")
    each_target(sum_four, part, "sent")
    each_target(sum_two, part, "sent")
    for c_ in stores:
        c_.wait()


def add_kernel(frac_ref, vel_ref, frac_off, vel_off, ofrac_ref, ovel_ref):
    ofrac_ref[...] = frac_ref[...] + frac_off[...][None, None]
    ovel_ref[...] = vel_ref[...] + vel_off[...][None, :, None]


def shards(fraction_levels, start_velocity, electrode_plan):
    line = (SUB, LANE)
    pad = (EXT, NZ + 2) + line
    flat = (EXT, NZ) + line
    row = (4,) + line

    def vmem(*shape):
        return pltpu.VMEM(shape, F32)

    end_fraction, end_velocity, fraction_off, velocity_off = pl.pallas_call(
        kernel,
        out_shape=(
            jax.ShapeDtypeStruct(fraction_levels.shape, F32),
            jax.ShapeDtypeStruct(start_velocity.shape, F32),
            jax.ShapeDtypeStruct(fraction_levels.shape[2:], F32),
            jax.ShapeDtypeStruct((3,) + fraction_levels.shape[2:], F32),
        ),
        in_specs=[
            pl.BlockSpec(memory_space=pl.ANY),
            pl.BlockSpec(memory_space=pl.ANY),
            pl.BlockSpec(memory_space=pltpu.SMEM),
        ],
        out_specs=(pl.BlockSpec(memory_space=pl.ANY),) * 4,
        scratch_shapes=[
            pltpu.VMEM((ROWS, NZ) + line, jnp.int32),
            vmem(*pad), vmem(*pad),
            vmem(3, *pad), vmem(3, *pad),
            vmem(EXT + 1, NZ, *line), vmem(*pad), vmem(*flat), vmem(*flat), vmem(*flat),
            vmem(*pad), vmem(*pad), vmem(*pad),
            vmem(FINE, 3, *line), vmem(NZ, *line),
            vmem(5, *row), vmem(*row), vmem(*row),
            vmem(5, *row), vmem(9, *row), vmem(13, *row), vmem(9, *row), vmem(17, *row),
            vmem(*row), vmem(17, *row), vmem(17, *row), vmem(4, NZ, *line),
            pltpu.SemaphoreType.DMA((2, ROWS, SUB)), pltpu.SemaphoreType.DMA((4, SUB)),
            pltpu.SemaphoreType.DMA((30, 2)), pltpu.SemaphoreType.DMA((30, 2)),
            pltpu.SemaphoreType.DMA((58,)), pltpu.SemaphoreType.DMA((58,)),
            pltpu.SemaphoreType.REGULAR((4,)),
        ],
        compiler_params=pltpu.CompilerParams(
            collective_id=0, has_side_effects=True, vmem_limit_bytes=62 * 2**20
        ),
    )(fraction_levels, start_velocity, electrode_plan)
    def frac(i):
        return 0, i, 0, 0

    def vel(i):
        return 0, 0, i, 0, 0

    layers, columns = fraction_levels.shape[2:]
    frac_spec = pl.BlockSpec((1, 2, layers, columns), frac)
    vel_spec = pl.BlockSpec((1, 3, 2, layers, columns), vel)
    return pl.pallas_call(
        add_kernel,
        grid=(ROWS // 2,),
        out_shape=(
            jax.ShapeDtypeStruct(end_fraction.shape, F32),
            jax.ShapeDtypeStruct(end_velocity.shape, F32),
        ),
        in_specs=[
            frac_spec, vel_spec,
            pl.BlockSpec((layers, columns), lambda i: (0, 0)),
            pl.BlockSpec((3, layers, columns), lambda i: (0, 0, 0)),
        ],
        out_specs=(frac_spec, vel_spec),
    )(end_fraction, end_velocity, fraction_off, velocity_off)


def solution(mesh):
    return jax.shard_map(
        shards,
        mesh=mesh,
        in_specs=(
            P("tm", "space", None, None),
            P("tm", None, "space", None, None),
            P("tm", None, None),
        ),
        out_specs=(P("tm", "space", None, None), P("tm", None, "space", None, None)),
        check_vma=False,
    )
```

```python
import functools

import jax
import jax.numpy as jnp
from jax import lax
from jax.experimental import pallas as pl
from jax.experimental.pallas import tpu as pltpu
from jax.sharding import PartitionSpec as P

MESH = pl.DeviceIdType.MESH
F32 = jnp.float32

ROWS = 4
NZ = 16
SUB, LANE = 8, 128
H = 4
EXT = ROWS + 2 * H
TILE = 32
TILES = 4
STRIPS = 32
FINE = 2
U = 16

SLICES, SPACE = 8, 32
wall_scale = 1.5 * 0.25 * 0.5
wall_decay = 4.0
level_scale = 1.0 / 1024.0
fraction_spread, velocity_spread = 0.05, 0.15


def lane_ids():
    sub = lax.broadcasted_iota(jnp.int32, (SUB, LANE), 0)
    lane = lax.broadcasted_iota(jnp.int32, (SUB, LANE), 1)
    return sub, lane


def roll(v, by, axis):
    return pltpu.roll(v, by, axis)


def next_y(v, masks, fill=0.0, by=1):
    ax = v.ndim
    r = roll(v, LANE - by, ax - 1)
    q = roll(r, SUB - 1, ax - 2)
    if fill is not None:
        q = jnp.where(masks["last_sub"], fill, q)
    return jnp.where(masks["last_lane"] if by == 1 else masks["last_group"], q, r)


def prev_y(v, masks, fill=0.0, by=1):
    ax = v.ndim
    r = roll(v, by, ax - 1)
    q = roll(r, 1, ax - 2)
    if fill is not None:
        q = jnp.where(masks["first_sub"], fill, q)
    return jnp.where(masks["first_lane"] if by == 1 else masks["first_group"], q, r)


def upwind(lower, upper, speed_lower, speed_upper):
    speed = speed_lower + speed_upper
    return speed * jnp.where(speed > 0.0, lower, upper)


def rho_of(c):
    return 0.1 + 0.9 * jnp.clip(c, 0.0, 1.0)


def kernel(
    lev_ref, vel_ref, plan_ref, ofrac_ref, ovel_ref, cfrac_ref, cvel_ref,
    levb, c_a, c_b, u, pv, gx, gz, gyl, gyu, rt, p1, p_a, p_b, elec, wall,
    cstart, prev, drive, rx1, rx2, rx3, rxs, rxq, part, w0, w1, wide,
    in_sem, out_sem, fs_send, fs_recv, cs_send, cs_recv, hand_sem,
):
    t = lax.axis_index("tm")
    s = lax.axis_index("space")
    sub, lane = lane_ids()
    masks = {
        "last_sub": sub == SUB - 1, "first_sub": sub == 0,
        "last_lane": lane == LANE - 1, "first_lane": lane == 0,
        "last_cell": (sub == SUB - 1) & (lane == LANE - 1), "first_cell": (sub == 0) & (lane == 0),
        "last_group": lane >= LANE - 4, "first_group": lane < 4,
    }

    def there(dt, ds):
        return (t + dt >= 0) & (t + dt < SLICES) & (s + ds >= 0) & (s + ds < SPACE)

    has_left, has_right = s > 0, s < SPACE - 1

    loads = {}
    for i in (0, ROWS - 1, 1, 2):
        loads[i] = []
        for k in range(SUB):
            cols = pl.ds(LANE * k, LANE)
            loads[i].append(pltpu.make_async_copy(
                lev_ref.at[0, i, :, cols], levb.at[i, :, k, :], in_sem.at[0, i, k]))
            loads[i].append(pltpu.make_async_copy(
                vel_ref.at[0, :, i, :, cols], u.at[:, H + i, pl.ds(1, NZ), k, :], in_sem.at[1, i, k]))
        for n, c in enumerate(loads[i]):
            c.start(priority=n // 2 % 2)

    zero_line = jnp.zeros((SUB, LANE), F32)
    cstart[...] = jnp.zeros(cstart.shape, F32)

    barrier = pltpu.get_barrier_semaphore()
    beside = [(0, 1), (0, -1), (1, 0), (-1, 0)]

    def tell(semaphore, places):
        for dt, ds in places:
            @pl.when(there(dt, ds))
            def _(dt=dt, ds=ds):
                pl.semaphore_signal(semaphore, inc=1, device_id=(t + dt, s + ds), device_id_type=MESH)

    def hear(semaphore, places):
        count = jnp.int32(0)
        for dt, ds in places:
            count = count + there(dt, ds).astype(jnp.int32)

        @pl.when(count > 0)
        def _():
            pl.semaphore_wait(semaphore, count)

    tell(barrier, beside)

    def zero_pads(e, _):
        for ref in (c_a, c_b, p1, p_a, p_b, pv.at[1], u.at[0], u.at[1], u.at[2]):
            ref[e, 0] = zero_line
            ref[e, NZ + 1] = zero_line
        return 0

    def zero_rows(first):
        def one(e, _):
            for ref in (c_a, c_b, p1, u.at[0], u.at[1], u.at[2]):
                ref[e] = jnp.zeros((NZ + 2, SUB, LANE), F32)
            return 0
        lax.fori_loop(first, first + H, one, 0)

    def fill_tables():
        lax.fori_loop(0, EXT, zero_pads, 0)

        @pl.when(s == 0)
        def _():
            zero_rows(0)

        @pl.when(s == SPACE - 1)
        def _():
            zero_rows(H + ROWS)

        for ref in (rx1, rx2, rx3, rxs, rxq):
            ref[...] = jnp.zeros(ref.shape, F32)
        strip = sub * 4 + lax.div(lane, TILE)
        tiles = [jnp.clip(lax.div(first_row - 1 + TILE, TILE) - 1, 0, TILES - 1), lax.div(first_row, TILE),
                 jnp.clip(lax.div(first_row + ROWS, TILE), 0, TILES - 1)]
        for f in range(FINE):
            def paint(q, fields, f=f):
                return tuple(jnp.where(strip == q, plan_ref[f, tile, q].astype(F32), field)
                             for tile, field in zip(tiles, fields))
            painted = lax.fori_loop(0, STRIPS, paint, (zero_line,) * 3, unroll=4)
            for j in range(3):
                elec[f, j] = painted[j]
        for z in range(NZ):
            wall[z] = jnp.full((SUB, LANE), wall_scale, F32) * jnp.exp(jnp.full((SUB, LANE), -z / wall_decay, F32))

    first_row = s * ROWS
    def load(i):
        for c in loads[i]:
            c.wait()
        c_a[H + i, pl.ds(1, NZ)] = levb[i].astype(F32) * level_scale

    load(0)
    load(ROWS - 1)
    hear(barrier, beside)

    def row_copies(entries, base):
        rights, lefts = [], []
        for n, (ref, skip, count) in enumerate(entries):
            first = H + ROWS - skip - count
            rights.append(pltpu.make_async_remote_copy(
                src_ref=ref.at[pl.ds(first, count), pl.ds(1, NZ)],
                dst_ref=ref.at[pl.ds(first - ROWS, count), pl.ds(1, NZ)],
                send_sem=fs_send.at[base + n, 0], recv_sem=fs_recv.at[base + n, 0],
                device_id=(t, s + 1), device_id_type=MESH))
            first = H + skip
            lefts.append(pltpu.make_async_remote_copy(
                src_ref=ref.at[pl.ds(first, count), pl.ds(1, NZ)],
                dst_ref=ref.at[pl.ds(first + ROWS, count), pl.ds(1, NZ)],
                send_sem=fs_send.at[base + n, 1], recv_sem=fs_recv.at[base + n, 1],
                device_id=(t, s - 1), device_id_type=MESH))
        return rights, lefts

    def start(copies):
        rights, lefts = copies

        @pl.when(has_right)
        def _():
            for c in rights:
                c.start()

        @pl.when(has_left)
        def _():
            for c in lefts:
                c.start()

    def landed(copies):
        rights, lefts = copies

        @pl.when(has_left)
        def _():
            for c in rights:
                c.wait_recv()

        @pl.when(has_right)
        def _():
            for c in lefts:
                c.wait_recv()

    def sent(copies):
        rights, lefts = copies

        @pl.when(has_right)
        def _():
            for c in rights:
                c.wait_send()

        @pl.when(has_left)
        def _():
            for c in lefts:
                c.wait_send()

    def coarse_copy(link, src, ds):
        dst, reach, dt, base, lo, hi = link
        j = reach - ds
        return pltpu.make_async_remote_copy(
            src_ref=src, dst_ref=dst.at[j], send_sem=cs_send.at[base + j], recv_sem=cs_recv.at[base + j],
            device_id=(t + dt, s + ds), device_id_type=MESH)

    def each_target(link, src, action):
        dst, reach, dt, base, lo, hi = link

        mine = (t >= lo) & (t <= hi)
        all_there = mine & (s >= reach) & (s < SPACE - reach)

        @pl.when(all_there)
        def _():
            for ds in range(-reach, reach + 1):
                if dt != 0 or ds != 0:
                    c = coarse_copy(link, src, ds)
                    c.start() if action == "start" else c.wait_send()

        @pl.when(mine & jnp.logical_not(all_there))
        def _():
            def one(j, _):
                ds = j - reach
                ok = there(dt, ds)
                if dt == 0:
                    ok = ok & (ds != 0)

                @pl.when(ok)
                def _():
                    c = coarse_copy(link, src, ds)
                    c.start() if action == "start" else c.wait_send()

                return 0
            lax.fori_loop(0, 2 * reach + 1, one, 0)

    def each_source(link, src):
        dst, reach, dt, base, lo, hi = link

        mine = (t - dt >= lo) & (t - dt <= hi)
        all_there = mine & (s >= reach) & (s < SPACE - reach)

        @pl.when(all_there)
        def _():
            for ds in range(-reach, reach + 1):
                if dt != 0 or ds != 0:
                    coarse_copy(link, src, ds).wait_recv()

        @pl.when(mine & jnp.logical_not(all_there))
        def _():
            def one(j, _):
                ds = reach - j
                ok = there(-dt, -ds)
                if dt == 0:
                    ok = ok & (ds != 0)

                @pl.when(ok)
                def _():
                    coarse_copy(link, src, ds).wait_recv()

                return 0
            lax.fori_loop(0, 2 * reach + 1, one, 0)

    starts = (cstart, 2, 0, 0, 0, SLICES - 1)
    one_back = (rx1, 2, 1, 5, 0, SLICES - 2)
    two_back = (rx2, 4, 2, 10, 0, SLICES - 3)
    three_back = (rx3, 6, 3, 19, 0, 0)
    sum_two = (rxs, 4, 2, 32, 2, 5)
    sum_four = (rxq, 8, 4, 41, 2, 3)

    def inside(row):
        return ((row >= 0) & (row < SPACE * ROWS)).astype(F32)

    def over(rows, body):
        lo, hi = rows

        def pair(j, _):
            body(lo + 2 * j, 0)
            body(lo + 2 * j + 1, 0)
            return 0
        lax.fori_loop(0, (hi - lo) // 2, pair, 0)

    def six(ref, e, z0):
        mid = ref[e, pl.ds(z0, U + 2)]
        return ref[e - 1, pl.ds(z0 + 1, U)], ref[e + 1, pl.ds(z0 + 1, U)], mid

    def advance(c, new_c, f, e, z0, which, full):
        cxm, cxp, cz = six(c, e, z0)
        uxm, uxp, uz = six(u.at[0], e, z0)
        c0, u0 = cz[1:-1], uz[1:-1]
        cym, cyp = prev_y(c0, masks), next_y(c0, masks)
        w = u[1, e, pl.ds(z0, U + 2)]
        v = u[2, e, pl.ds(z0 + 1, U)]
        vm, vp = prev_y(v, masks), next_y(v, masks)
        net = upwind(c0, cxp, u0, uxp) - upwind(cxm, c0, uxm, u0)
        fz = upwind(cz[:-1], cz[1:], w[:-1], w[1:])
        net = net + (fz[1:] - fz[:-1])
        net = net + (upwind(c0, cyp, v, vp) - upwind(cym, c0, vm, v))
        fresh = c0 - 0.125 * net
        pull = elec[f, which] * wall[pl.ds(z0, U)] / rho_of(c0)
        around = uxm + uxp + uz[:-2] + uz[2:] + prev_y(u0, masks) + next_y(u0, masks)
        px = 0.85 * u0 + (0.025 * around + pull * (cxp - cxm))
        if not full:
            keep = inside(first_row + e - H)
            fresh = fresh * keep
            px = px * keep
        new_c[e, pl.ds(z0 + 1, U)] = fresh
        pv[0, e, pl.ds(z0 + 1, U)] = px
        if full:
            wxm, wxp = u[1, e - 1, pl.ds(z0 + 1, U)], u[1, e + 1, pl.ds(z0 + 1, U)]
            w0_ = w[1:-1]
            around = wxm + wxp + w[:-2] + w[2:] + prev_y(w0_, masks) + next_y(w0_, masks)
            pv[1, e, pl.ds(z0 + 1, U)] = 0.85 * w0_ + (0.025 * around + pull * (cz[2:] - cz[:-2]))
            vxm, vxp, vz = six(u.at[2], e, z0)
            around = vxm + vxp + vz[:-2] + vz[2:] + vm + vp
            pv[2, e, pl.ds(z0 + 1, U)] = 0.85 * v + (0.025 * around + pull * (cyp - cym))

    def face_block(new_c, e, z0, top):
        rz = rho_of(new_c[e, pl.ds(z0, U + 2)])
        r0 = rz[1:-1]
        rxm = rho_of(new_c[e - 1, pl.ds(z0 + 1, U)])
        rxp = rho_of(new_c[e + 1, pl.ds(z0 + 1, U)])
        lower = 1.0 / (rxm + r0)
        upper = 1.0 / (rxp + r0)
        gx[e, pl.ds(z0, U)] = lower
        gx[e + 1, pl.ds(z0, U)] = upper
        zface = 1.0 / (rz[:-1] + rz[1:])
        gz[e, pl.ds(z0, U + 1)] = zface
        yl = 1.0 / (r0 + prev_y(r0, masks, 0.1))
        yu = 1.0 / (r0 + next_y(r0, masks, 0.1))
        gyl[e, pl.ds(z0, U)] = jnp.where(masks["first_cell"], 0.0, yl)
        gyu[e, pl.ds(z0, U)] = jnp.where(masks["last_cell"], 0.0, yu)
        total = lower + upper + (zface[:-1] + zface[1:]) + (yl + yu)
        inverse = 1.0 / total
        if not top:
            inverse = inverse * inside(first_row + e - H)
        rt[e, pl.ds(z0, U)] = inverse
        return inverse

    def first_pressure(new_c, e, z0):
        inverse = face_block(new_c, e, z0, True)
        pz = pv[1, e, pl.ds(z0, U + 2)]
        py = pv[2, e, pl.ds(z0 + 1, U)]
        source = pv[0, e + 1, pl.ds(z0 + 1, U)] - pv[0, e - 1, pl.ds(z0 + 1, U)]
        source = source + (pz[2:] - pz[:-2]) + (next_y(py, masks) - prev_y(py, masks))
        p1[e, pl.ds(z0 + 1, U)] = -(source * inverse)

    def sweep(old, new, e, z0):
        pxm, pxp, pz = six(old, e, z0)
        p0 = pz[1:-1]
        zface = gz[e, pl.ds(z0, U + 1)]
        summed = gx[e, pl.ds(z0, U)] * pxm + gx[e + 1, pl.ds(z0, U)] * pxp
        summed = summed + (zface[:-1] * pz[:-2] + zface[1:] * pz[2:])
        summed = summed + (gyl[e, pl.ds(z0, U)] * prev_y(p0, masks, None) + gyu[e, pl.ds(z0, U)] * next_y(p0, masks, None))
        new[e, pl.ds(z0 + 1, U)] = p1[e, pl.ds(z0 + 1, U)] + rt[e, pl.ds(z0, U)] * summed

    def project(new_c, e, z0):
        pxm, pxp, pz = six(p_a, e, z0)
        p0 = pz[1:-1]
        scale = 0.125 / rho_of(new_c[e, pl.ds(z0 + 1, U)])
        zs = pl.ds(z0 + 1, U)
        u[0, e, zs] = pv[0, e, zs] - scale * (pxp - pxm)
        u[1, e, zs] = pv[1, e, zs] - scale * (pz[2:] - pz[:-2])
        u[2, e, zs] = pv[2, e, zs] - scale * (next_y(p0, masks) - prev_y(p0, masks))

    even, low = lax.rem(lane, 2) == 0, lax.rem(lane, 4) < 2
    spread = jnp.where(lax.rem(lane, 4) == 0, fraction_spread, velocity_spread).astype(F32)

    def combine(a, b, by, mask):
        keep, other = jnp.where(mask, a, b), jnp.where(mask, b, a)
        return keep + jnp.where(mask, roll(other, LANE - by, 2), roll(other, by, 2))

    def restrict(c, out):
        sums = []
        for ref in (c, u.at[0], u.at[1], u.at[2]):
            total = None
            for i in range(ROWS):
                part = ref[H + i, pl.ds(1, NZ)]
                total = part if total is None else total + part
            sums.append(jnp.sum(total.reshape(4, 4, SUB, LANE), axis=1))
        pair = combine(sums[0], sums[1], 1, even), combine(sums[2], sums[3], 1, even)
        out[...] = combine(pair[0], pair[1], 2, low) * (1.0 / 64.0)

    def diffuse(src, dst, length, out_reach):
        whole = src[pl.ds(0, length + 2)]
        v = whole[1:-1]
        edge = jnp.zeros((length, 1, SUB, LANE), F32)
        up = jnp.concatenate([v[:, 1:], edge], axis=1)
        down = jnp.concatenate([edge, v[:, :-1]], axis=1)
        around = whole[:-2] + whole[2:] + up + down + next_y(v, masks, by=4) + prev_y(v, masks, by=4)
        fresh = v + spread * (around - 6.0 * v)
        for j in range(length):
            row = s + j - out_reach
            keep = ((row >= 0) & (row < SPACE)).astype(F32)
            dst[j] = fresh[j] * keep

    def diffuse_down(src, reach, steps):
        now = src
        for step in range(steps):
            reach -= 1
            target = w0 if step % 2 == 0 else w1
            diffuse(now, target, 2 * reach + 1, reach)
            now = target
        return now

    near = row_copies([(c_a, 0, 1), (u.at[0], 0, 1), (u.at[1], 0, 1), (u.at[2], 0, 1)], 0)
    far = row_copies([(c_a, 1, 1), (u.at[0], 1, 1)], 4)
    start(near)
    load(1)
    load(2)
    start(far)
    tell(hand_sem.at[0], [(1, 0), (-1, 0)])
    fill_tables()
    restrict(c_a, cstart.at[2])

    def both(body, *rows):
        for e in rows:
            body(e, 0)

    c, new_c = c_a, c_b
    last = H + ROWS - 1
    for f in range(FINE):
        def step_full(e, z0):
            advance(c, new_c, f, e, z0, 1, True)

        def faces(e, z0):
            face_block(new_c, e, z0, False)

        def first_p(e, z0):
            first_pressure(new_c, e, z0)

        def sweep_1(e, z0):
            sweep(p1, p_a, e, z0)

        def sweep_2(e, z0):
            sweep(p_a, p_b, e, z0)

        def sweep_3(e, z0):
            sweep(p_b, p_a, e, z0)

        base = 6 + 10 * f
        over((H + 1, last), step_full)
        fraction_mid = row_copies([(new_c, 1, 2)], base)
        start(fraction_mid)
        landed(near)
        both(step_full, H, last)
        fraction_far = row_copies([(new_c, 3, 1)], base + 1)
        start(fraction_far)
        over((H + 1, last), first_p)
        pressure_mid = row_copies([(p1, 1, 2)], base + 2)
        start(pressure_mid)
        if f == 0:
            hear(hand_sem.at[0], [(1, 0), (-1, 0)])
            tell(hand_sem.at[1], [(2, 0), (-2, 0)])
            each_target(starts, cstart.at[2], "start")
        else:
            hear(hand_sem.at[1], [(2, 0), (-2, 0)])
            tell(hand_sem.at[2], [(0, 4), (0, -4)])
        landed(far)
        advance(c, new_c, f, H - 1, 0, 0, False)
        advance(c, new_c, f, last + 1, 0, 2, False)
        both(first_p, H, last)
        pressure_near = row_copies([(p1, 0, 1)], base + 3)
        pressure_far = row_copies([(p1, 3, 1)], base + 4)
        start(pressure_near)
        start(pressure_far)
        over((H + 1, last), sweep_1)
        landed(fraction_mid)
        both(faces, H - 1, last + 1)
        landed(fraction_far)
        both(faces, H - 2, last + 2)
        both(faces, H - 3, last + 3)
        if f == 0:
            each_source(starts, cstart.at[2])
            done = diffuse_down(cstart, 2, 2)
            prev[...] = done[0] * (t > 0).astype(F32)
        else:
            hear(hand_sem.at[2], [(0, 4), (0, -4)])
            tell(hand_sem.at[3], [(-k, 0) for k in (1, 2, 3, 4)])
        landed(pressure_mid)
        landed(pressure_near)
        both(sweep_1, H, last)
        both(sweep_1, H - 1, last + 1)
        both(sweep_1, H - 2, last + 2)
        over((H - 1, last + 2), sweep_2)
        over((H, last + 1), sweep_3)
        landed(pressure_far)
        both(sweep_1, H - 3, last + 3)
        both(sweep_2, H - 2, last + 2)
        both(sweep_3, H - 1, last + 1)
        sent(near)
        sent(far)
        def end(e, z0):
            project(new_c, e, z0)

        both(end, H, last)
        if f == 0:
            near = row_copies([(u.at[0], 0, 1), (u.at[1], 0, 1), (u.at[2], 0, 1)], 26)
            start(near)
        over((H + 1, last), end)
        if f == 0:
            far = row_copies([(u.at[0], 1, 1)], 29)
            start(far)
        for copies in (fraction_mid, fraction_far, pressure_mid, pressure_near, pressure_far):
            sent(copies)
        c, new_c = new_c, c
    each_target(starts, cstart.at[2], "sent")

    stores = []
    for k in range(SUB):
        cols = pl.ds(LANE * k, LANE)
        stores.append(pltpu.make_async_copy(
            c.at[pl.ds(H, ROWS), pl.ds(1, NZ), k, :], ofrac_ref.at[0, :, :, cols], out_sem.at[0, k]))
        stores.append(pltpu.make_async_copy(
            u.at[:, pl.ds(H, ROWS), pl.ds(1, NZ), k, :], ovel_ref.at[0, :, :, :, cols], out_sem.at[1, k]))
    restrict(c, drive)
    drive[...] = drive[...] - prev[...]
    hear(hand_sem.at[3], [(k, 0) for k in (1, 2, 3, 4)])
    each_target(three_back, drive, "start")
    each_target(two_back, drive, "start")
    each_target(one_back, drive, "start")
    for c_ in stores:
        c_.start()
    each_source(three_back, drive)
    three = diffuse_down(rx3, 6, 2)
    each_source(two_back, drive)
    three[pl.ds(0, 9)] = three[pl.ds(0, 9)] + rx2[...]
    diffuse(three, w0, 7, 3)
    diffuse(w0, w1, 5, 2)
    each_source(one_back, drive)
    w1[pl.ds(0, 5)] = w1[pl.ds(0, 5)] + rx1[...]
    diffuse(w1, w0, 3, 1)
    diffuse(w0, w1, 1, 0)
    part[...] = w1[0]
    each_target(sum_four, part, "start")
    each_target(sum_two, part, "start")
    each_source(sum_four, part)
    eight = diffuse_down(rxq, 8, 4)
    each_source(sum_two, part)
    eight[pl.ds(0, 9)] = eight[pl.ds(0, 9)] + rxs[...]
    four = diffuse_down(eight, 4, 4)
    correction = (part[...] + four[0]) - prev[...]

    for field in range(4):
        m = jnp.where(lax.rem(lane, 4) == field, correction, 0.0)
        m = m + roll(m, 1 if field % 2 == 0 else LANE - 1, 2)
        m = m + roll(m, 2 if field < 2 else LANE - 2, 2)
        wide[field] = jnp.broadcast_to(m[:, None], (4, 4, SUB, LANE)).reshape(NZ, SUB, LANE)
    for k in range(SUB):
        cols = pl.ds(LANE * k, LANE)
        stores.append(pltpu.make_async_copy(wide.at[0, :, k, :], cfrac_ref.at[:, cols], out_sem.at[2, k]))
        stores.append(pltpu.make_async_copy(wide.at[1:4, :, k, :], cvel_ref.at[:, :, cols], out_sem.at[3, k]))
        stores[-2].start()
        stores[-1].start(priority=1)
    each_target(three_back, drive, "sent")
    each_target(two_back, drive, "sent")
    each_target(one_back, drive, "sent")
    each_target(sum_four, part, "sent")
    each_target(sum_two, part, "sent")
    for c_ in stores:
        c_.wait()


def add_kernel(frac_ref, vel_ref, frac_off, vel_off, ofrac_ref, ovel_ref):
    ofrac_ref[...] = frac_ref[...] + frac_off[...][None, None]
    ovel_ref[...] = vel_ref[...] + vel_off[...][None, :, None]


def shards(fraction_levels, start_velocity, electrode_plan):
    line = (SUB, LANE)
    pad = (EXT, NZ + 2) + line
    flat = (EXT, NZ) + line
    row = (4,) + line

    def vmem(*shape):
        return pltpu.VMEM(shape, F32)

    end_fraction, end_velocity, fraction_off, velocity_off = pl.pallas_call(
        kernel,
        out_shape=(
            jax.ShapeDtypeStruct(fraction_levels.shape, F32),
            jax.ShapeDtypeStruct(start_velocity.shape, F32),
            jax.ShapeDtypeStruct(fraction_levels.shape[2:], F32),
            jax.ShapeDtypeStruct((3,) + fraction_levels.shape[2:], F32),
        ),
        in_specs=[
            pl.BlockSpec(memory_space=pl.ANY),
            pl.BlockSpec(memory_space=pl.ANY),
            pl.BlockSpec(memory_space=pltpu.SMEM),
        ],
        out_specs=(pl.BlockSpec(memory_space=pl.ANY),) * 4,
        scratch_shapes=[
            pltpu.VMEM((ROWS, NZ) + line, jnp.int32),
            vmem(*pad), vmem(*pad),
            vmem(3, *pad), vmem(3, *pad),
            vmem(EXT + 1, NZ, *line), vmem(*pad), vmem(*flat), vmem(*flat), vmem(*flat),
            vmem(*pad), vmem(*pad), vmem(*pad),
            vmem(FINE, 3, *line), vmem(NZ, *line),
            vmem(5, *row), vmem(*row), vmem(*row),
            vmem(5, *row), vmem(9, *row), vmem(13, *row), vmem(9, *row), vmem(17, *row),
            vmem(*row), vmem(17, *row), vmem(17, *row), vmem(4, NZ, *line),
            pltpu.SemaphoreType.DMA((2, ROWS, SUB)), pltpu.SemaphoreType.DMA((4, SUB)),
            pltpu.SemaphoreType.DMA((30, 2)), pltpu.SemaphoreType.DMA((30, 2)),
            pltpu.SemaphoreType.DMA((58,)), pltpu.SemaphoreType.DMA((58,)),
            pltpu.SemaphoreType.REGULAR((4,)),
        ],
        compiler_params=pltpu.CompilerParams(
            collective_id=0, has_side_effects=True, vmem_limit_bytes=62 * 2**20
        ),
    )(fraction_levels, start_velocity, electrode_plan)
    def frac(i):
        return 0, i, 0, 0

    def vel(i):
        return 0, 0, i, 0, 0

    layers, columns = fraction_levels.shape[2:]
    frac_spec = pl.BlockSpec((1, 2, layers, columns), frac)
    vel_spec = pl.BlockSpec((1, 3, 2, layers, columns), vel)
    return pl.pallas_call(
        add_kernel,
        grid=(ROWS // 2,),
        out_shape=(
            jax.ShapeDtypeStruct(end_fraction.shape, F32),
            jax.ShapeDtypeStruct(end_velocity.shape, F32),
        ),
        in_specs=[
            frac_spec, vel_spec,
            pl.BlockSpec((layers, columns), lambda i: (0, 0)),
            pl.BlockSpec((3, layers, columns), lambda i: (0, 0, 0)),
        ],
        out_specs=(frac_spec, vel_spec),
    )(end_fraction, end_velocity, fraction_off, velocity_off)


def solution(mesh):
    return jax.shard_map(
        shards,
        mesh=mesh,
        in_specs=(
            P("tm", "space", None, None),
            P("tm", None, "space", None, None),
            P("tm", None, None),
        ),
        out_specs=(P("tm", "space", None, None), P("tm", None, "space", None, None)),
        check_vma=False,
    )
```

```python
import functools

import jax
import jax.numpy as jnp
from jax import lax
from jax.experimental import pallas as pl
from jax.experimental.pallas import tpu as pltpu
from jax.sharding import PartitionSpec as P

MESH = pl.DeviceIdType.MESH
F32 = jnp.float32

ROWS = 4
NZ = 16
SUB, LANE = 8, 128
H = 4
EXT = ROWS + 2 * H
TILE = 32
TILES = 4
STRIPS = 32
FINE = 2
U = 16

SLICES, SPACE = 8, 32
wall_scale = 1.5 * 0.25 * 0.5
wall_decay = 4.0
level_scale = 1.0 / 1024.0
fraction_spread, velocity_spread = 0.05, 0.15


def lane_ids():
    sub = lax.broadcasted_iota(jnp.int32, (SUB, LANE), 0)
    lane = lax.broadcasted_iota(jnp.int32, (SUB, LANE), 1)
    return sub, lane


def roll(v, by, axis):
    return pltpu.roll(v, by, axis)


def next_y(v, masks, fill=0.0, by=1):
    ax = v.ndim
    r = roll(v, LANE - by, ax - 1)
    q = roll(r, SUB - 1, ax - 2)
    if fill is not None:
        q = jnp.where(masks["last_sub"], fill, q)
    return jnp.where(masks["last_lane"] if by == 1 else masks["last_group"], q, r)


def prev_y(v, masks, fill=0.0, by=1):
    ax = v.ndim
    r = roll(v, by, ax - 1)
    q = roll(r, 1, ax - 2)
    if fill is not None:
        q = jnp.where(masks["first_sub"], fill, q)
    return jnp.where(masks["first_lane"] if by == 1 else masks["first_group"], q, r)


def upwind(lower, upper, speed_lower, speed_upper):
    speed = speed_lower + speed_upper
    return speed * jnp.where(speed > 0.0, lower, upper)


def rho_of(c):
    return 0.1 + 0.9 * jnp.clip(c, 0.0, 1.0)


def kernel(
    lev_ref, vel_ref, plan_ref, ofrac_ref, ovel_ref, cfrac_ref, cvel_ref,
    levb, c_a, c_b, u, pv, gx, gz, gyl, gyu, rt, p1, p_a, p_b, elec, wall,
    cstart, prev, drive, rx1, rx2, rx3, rxs, rxq, part, w0, w1, wide,
    in_sem, out_sem, fs_send, fs_recv, cs_send, cs_recv, hand_sem,
):
    t = lax.axis_index("tm")
    s = lax.axis_index("space")
    sub, lane = lane_ids()
    masks = {
        "last_sub": sub == SUB - 1, "first_sub": sub == 0,
        "last_lane": lane == LANE - 1, "first_lane": lane == 0,
        "last_cell": (sub == SUB - 1) & (lane == LANE - 1), "first_cell": (sub == 0) & (lane == 0),
        "last_group": lane >= LANE - 4, "first_group": lane < 4,
    }

    def there(dt, ds):
        return (t + dt >= 0) & (t + dt < SLICES) & (s + ds >= 0) & (s + ds < SPACE)

    has_left, has_right = s > 0, s < SPACE - 1

    loads = {}
    for i in (0, ROWS - 1, 1, 2):
        loads[i] = []
        for k in range(SUB):
            cols = pl.ds(LANE * k, LANE)
            loads[i].append(pltpu.make_async_copy(
                lev_ref.at[0, i, :, cols], levb.at[i, :, k, :], in_sem.at[0, i, k]))
            loads[i].append(pltpu.make_async_copy(
                vel_ref.at[0, :, i, :, cols], u.at[:, H + i, pl.ds(1, NZ), k, :], in_sem.at[1, i, k]))
        for n, c in enumerate(loads[i]):
            c.start(priority=n // 2 % 2)

    zero_line = jnp.zeros((SUB, LANE), F32)
    cstart[...] = jnp.zeros(cstart.shape, F32)

    barrier = pltpu.get_barrier_semaphore()
    beside = [(0, 1), (0, -1), (1, 0), (-1, 0)]

    def tell(semaphore, places):
        for dt, ds in places:
            @pl.when(there(dt, ds))
            def _(dt=dt, ds=ds):
                pl.semaphore_signal(semaphore, inc=1, device_id=(t + dt, s + ds), device_id_type=MESH)

    def hear(semaphore, places):
        count = jnp.int32(0)
        for dt, ds in places:
            count = count + there(dt, ds).astype(jnp.int32)

        @pl.when(count > 0)
        def _():
            pl.semaphore_wait(semaphore, count)

    tell(barrier, beside)

    def zero_pads(e, _):
        for ref in (c_a, c_b, p1, p_a, p_b, pv.at[1], u.at[0], u.at[1], u.at[2]):
            ref[e, 0] = zero_line
            ref[e, NZ + 1] = zero_line
        return 0

    def zero_rows(first):
        def one(e, _):
            for ref in (c_a, c_b, p1, u.at[0], u.at[1], u.at[2]):
                ref[e] = jnp.zeros((NZ + 2, SUB, LANE), F32)
            return 0
        lax.fori_loop(first, first + H, one, 0)

    def fill_tables():
        lax.fori_loop(0, EXT, zero_pads, 0)

        @pl.when(s == 0)
        def _():
            zero_rows(0)

        @pl.when(s == SPACE - 1)
        def _():
            zero_rows(H + ROWS)

        for ref in (rx1, rx2, rx3, rxs, rxq):
            ref[...] = jnp.zeros(ref.shape, F32)
        strip = sub * 4 + lax.div(lane, TILE)
        tiles = [jnp.clip(lax.div(first_row - 1 + TILE, TILE) - 1, 0, TILES - 1), lax.div(first_row, TILE),
                 jnp.clip(lax.div(first_row + ROWS, TILE), 0, TILES - 1)]
        for f in range(FINE):
            def paint(q, fields, f=f):
                return tuple(jnp.where(strip == q, plan_ref[f, tile, q].astype(F32), field)
                             for tile, field in zip(tiles, fields))
            painted = lax.fori_loop(0, STRIPS, paint, (zero_line,) * 3, unroll=4)
            for j in range(3):
                elec[f, j] = painted[j]
        for z in range(NZ):
            wall[z] = jnp.full((SUB, LANE), wall_scale, F32) * jnp.exp(jnp.full((SUB, LANE), -z / wall_decay, F32))

    first_row = s * ROWS
    def load(i):
        for c in loads[i]:
            c.wait()
        c_a[H + i, pl.ds(1, NZ)] = levb[i].astype(F32) * level_scale

    load(0)
    load(ROWS - 1)
    hear(barrier, beside)

    def row_copies(entries, base):
        rights, lefts = [], []
        for n, (ref, skip, count) in enumerate(entries):
            first = H + ROWS - skip - count
            rights.append(pltpu.make_async_remote_copy(
                src_ref=ref.at[pl.ds(first, count), pl.ds(1, NZ)],
                dst_ref=ref.at[pl.ds(first - ROWS, count), pl.ds(1, NZ)],
                send_sem=fs_send.at[base + n, 0], recv_sem=fs_recv.at[base + n, 0],
                device_id=(t, s + 1), device_id_type=MESH))
            first = H + skip
            lefts.append(pltpu.make_async_remote_copy(
                src_ref=ref.at[pl.ds(first, count), pl.ds(1, NZ)],
                dst_ref=ref.at[pl.ds(first + ROWS, count), pl.ds(1, NZ)],
                send_sem=fs_send.at[base + n, 1], recv_sem=fs_recv.at[base + n, 1],
                device_id=(t, s - 1), device_id_type=MESH))
        return rights, lefts

    def start(copies):
        rights, lefts = copies

        @pl.when(has_right)
        def _():
            for c in rights:
                c.start()

        @pl.when(has_left)
        def _():
            for c in lefts:
                c.start()

    def landed(copies):
        rights, lefts = copies

        @pl.when(has_left)
        def _():
            for c in rights:
                c.wait_recv()

        @pl.when(has_right)
        def _():
            for c in lefts:
                c.wait_recv()

    def sent(copies):
        rights, lefts = copies

        @pl.when(has_right)
        def _():
            for c in rights:
                c.wait_send()

        @pl.when(has_left)
        def _():
            for c in lefts:
                c.wait_send()

    def coarse_copy(link, src, ds):
        dst, reach, dt, base, lo, hi = link
        j = reach - ds
        return pltpu.make_async_remote_copy(
            src_ref=src, dst_ref=dst.at[j], send_sem=cs_send.at[base + j], recv_sem=cs_recv.at[base + j],
            device_id=(t + dt, s + ds), device_id_type=MESH)

    def each_target(link, src, action):
        dst, reach, dt, base, lo, hi = link

        mine = (t >= lo) & (t <= hi)
        all_there = mine & (s >= reach) & (s < SPACE - reach)

        @pl.when(all_there)
        def _():
            for ds in range(-reach, reach + 1):
                if dt != 0 or ds != 0:
                    c = coarse_copy(link, src, ds)
                    c.start() if action == "start" else c.wait_send()

        @pl.when(mine & jnp.logical_not(all_there))
        def _():
            def one(j, _):
                ds = j - reach
                ok = there(dt, ds)
                if dt == 0:
                    ok = ok & (ds != 0)

                @pl.when(ok)
                def _():
                    c = coarse_copy(link, src, ds)
                    c.start() if action == "start" else c.wait_send()

                return 0
            lax.fori_loop(0, 2 * reach + 1, one, 0)

    def each_source(link, src):
        dst, reach, dt, base, lo, hi = link

        mine = (t - dt >= lo) & (t - dt <= hi)
        all_there = mine & (s >= reach) & (s < SPACE - reach)

        @pl.when(all_there)
        def _():
            for ds in range(-reach, reach + 1):
                if dt != 0 or ds != 0:
                    coarse_copy(link, src, ds).wait_recv()

        @pl.when(mine & jnp.logical_not(all_there))
        def _():
            def one(j, _):
                ds = reach - j
                ok = there(-dt, -ds)
                if dt == 0:
                    ok = ok & (ds != 0)

                @pl.when(ok)
                def _():
                    coarse_copy(link, src, ds).wait_recv()

                return 0
            lax.fori_loop(0, 2 * reach + 1, one, 0)

    starts = (cstart, 2, 0, 0, 0, SLICES - 1)
    one_back = (rx1, 2, 1, 5, 0, SLICES - 2)
    two_back = (rx2, 4, 2, 10, 0, SLICES - 3)
    three_back = (rx3, 6, 3, 19, 0, 0)
    sum_two = (rxs, 4, 2, 32, 2, 5)
    sum_four = (rxq, 8, 4, 41, 2, 3)

    def inside(row):
        return ((row >= 0) & (row < SPACE * ROWS)).astype(F32)

    def over(rows, body):
        lo, hi = rows

        def pair(j, _):
            body(lo + 2 * j, 0)
            body(lo + 2 * j + 1, 0)
            return 0
        lax.fori_loop(0, (hi - lo) // 2, pair, 0)

    def six(ref, e, z0):
        mid = ref[e, pl.ds(z0, U + 2)]
        return ref[e - 1, pl.ds(z0 + 1, U)], ref[e + 1, pl.ds(z0 + 1, U)], mid

    def advance(c, new_c, f, e, z0, which, full):
        cxm, cxp, cz = six(c, e, z0)
        uxm, uxp, uz = six(u.at[0], e, z0)
        c0, u0 = cz[1:-1], uz[1:-1]
        cym, cyp = prev_y(c0, masks), next_y(c0, masks)
        w = u[1, e, pl.ds(z0, U + 2)]
        v = u[2, e, pl.ds(z0 + 1, U)]
        vm, vp = prev_y(v, masks), next_y(v, masks)
        net = upwind(c0, cxp, u0, uxp) - upwind(cxm, c0, uxm, u0)
        fz = upwind(cz[:-1], cz[1:], w[:-1], w[1:])
        net = net + (fz[1:] - fz[:-1])
        net = net + (upwind(c0, cyp, v, vp) - upwind(cym, c0, vm, v))
        fresh = c0 - 0.125 * net
        pull = elec[f, which] * wall[pl.ds(z0, U)] / rho_of(c0)
        around = uxm + uxp + uz[:-2] + uz[2:] + prev_y(u0, masks) + next_y(u0, masks)
        px = 0.85 * u0 + (0.025 * around + pull * (cxp - cxm))
        if not full:
            keep = inside(first_row + e - H)
            fresh = fresh * keep
            px = px * keep
        new_c[e, pl.ds(z0 + 1, U)] = fresh
        pv[0, e, pl.ds(z0 + 1, U)] = px
        if full:
            wxm, wxp = u[1, e - 1, pl.ds(z0 + 1, U)], u[1, e + 1, pl.ds(z0 + 1, U)]
            w0_ = w[1:-1]
            around = wxm + wxp + w[:-2] + w[2:] + prev_y(w0_, masks) + next_y(w0_, masks)
            pv[1, e, pl.ds(z0 + 1, U)] = 0.85 * w0_ + (0.025 * around + pull * (cz[2:] - cz[:-2]))
            vxm, vxp, vz = six(u.at[2], e, z0)
            around = vxm + vxp + vz[:-2] + vz[2:] + vm + vp
            pv[2, e, pl.ds(z0 + 1, U)] = 0.85 * v + (0.025 * around + pull * (cyp - cym))

    def face_block(new_c, e, z0, top):
        rz = rho_of(new_c[e, pl.ds(z0, U + 2)])
        r0 = rz[1:-1]
        rxm = rho_of(new_c[e - 1, pl.ds(z0 + 1, U)])
        rxp = rho_of(new_c[e + 1, pl.ds(z0 + 1, U)])
        lower = 1.0 / (rxm + r0)
        upper = 1.0 / (rxp + r0)
        gx[e, pl.ds(z0, U)] = lower
        gx[e + 1, pl.ds(z0, U)] = upper
        zface = 1.0 / (rz[:-1] + rz[1:])
        gz[e, pl.ds(z0, U + 1)] = zface
        yl = 1.0 / (r0 + prev_y(r0, masks, 0.1))
        yu = 1.0 / (r0 + next_y(r0, masks, 0.1))
        gyl[e, pl.ds(z0, U)] = jnp.where(masks["first_cell"], 0.0, yl)
        gyu[e, pl.ds(z0, U)] = jnp.where(masks["last_cell"], 0.0, yu)
        total = lower + upper + (zface[:-1] + zface[1:]) + (yl + yu)
        inverse = 1.0 / total
        if not top:
            inverse = inverse * inside(first_row + e - H)
        rt[e, pl.ds(z0, U)] = inverse
        return inverse

    def first_pressure(new_c, e, z0):
        inverse = face_block(new_c, e, z0, True)
        pz = pv[1, e, pl.ds(z0, U + 2)]
        py = pv[2, e, pl.ds(z0 + 1, U)]
        source = pv[0, e + 1, pl.ds(z0 + 1, U)] - pv[0, e - 1, pl.ds(z0 + 1, U)]
        source = source + (pz[2:] - pz[:-2]) + (next_y(py, masks) - prev_y(py, masks))
        p1[e, pl.ds(z0 + 1, U)] = -(source * inverse)

    def sweep(old, new, e, z0):
        pxm, pxp, pz = six(old, e, z0)
        p0 = pz[1:-1]
        zface = gz[e, pl.ds(z0, U + 1)]
        summed = gx[e, pl.ds(z0, U)] * pxm + gx[e + 1, pl.ds(z0, U)] * pxp
        summed = summed + (zface[:-1] * pz[:-2] + zface[1:] * pz[2:])
        summed = summed + (gyl[e, pl.ds(z0, U)] * prev_y(p0, masks, None) + gyu[e, pl.ds(z0, U)] * next_y(p0, masks, None))
        new[e, pl.ds(z0 + 1, U)] = p1[e, pl.ds(z0 + 1, U)] + rt[e, pl.ds(z0, U)] * summed

    def project(new_c, e, z0):
        pxm, pxp, pz = six(p_a, e, z0)
        p0 = pz[1:-1]
        scale = 0.125 / rho_of(new_c[e, pl.ds(z0 + 1, U)])
        zs = pl.ds(z0 + 1, U)
        u[0, e, zs] = pv[0, e, zs] - scale * (pxp - pxm)
        u[1, e, zs] = pv[1, e, zs] - scale * (pz[2:] - pz[:-2])
        u[2, e, zs] = pv[2, e, zs] - scale * (next_y(p0, masks) - prev_y(p0, masks))

    even, low = lax.rem(lane, 2) == 0, lax.rem(lane, 4) < 2
    spread = jnp.where(lax.rem(lane, 4) == 0, fraction_spread, velocity_spread).astype(F32)

    def combine(a, b, by, mask):
        keep, other = jnp.where(mask, a, b), jnp.where(mask, b, a)
        return keep + jnp.where(mask, roll(other, LANE - by, 2), roll(other, by, 2))

    def restrict(c, out):
        sums = []
        for ref in (c, u.at[0], u.at[1], u.at[2]):
            total = None
            for i in range(ROWS):
                part = ref[H + i, pl.ds(1, NZ)]
                total = part if total is None else total + part
            sums.append(jnp.sum(total.reshape(4, 4, SUB, LANE), axis=1))
        pair = combine(sums[0], sums[1], 1, even), combine(sums[2], sums[3], 1, even)
        out[...] = combine(pair[0], pair[1], 2, low) * (1.0 / 64.0)

    def diffuse(src, dst, length, out_reach):
        whole = src[pl.ds(0, length + 2)]
        v = whole[1:-1]
        edge = jnp.zeros((length, 1, SUB, LANE), F32)
        up = jnp.concatenate([v[:, 1:], edge], axis=1)
        down = jnp.concatenate([edge, v[:, :-1]], axis=1)
        around = whole[:-2] + whole[2:] + up + down + next_y(v, masks, by=4) + prev_y(v, masks, by=4)
        fresh = v + spread * (around - 6.0 * v)
        for j in range(length):
            row = s + j - out_reach
            keep = ((row >= 0) & (row < SPACE)).astype(F32)
            dst[j] = fresh[j] * keep

    def diffuse_down(src, reach, steps):
        now = src
        for step in range(steps):
            reach -= 1
            target = w0 if step % 2 == 0 else w1
            diffuse(now, target, 2 * reach + 1, reach)
            now = target
        return now

    near = row_copies([(c_a, 0, 1), (u.at[0], 0, 1), (u.at[1], 0, 1), (u.at[2], 0, 1)], 0)
    far = row_copies([(c_a, 1, 1), (u.at[0], 1, 1)], 4)
    start(near)
    load(1)
    load(2)
    start(far)
    tell(hand_sem.at[0], [(1, 0), (-1, 0)])
    fill_tables()
    restrict(c_a, cstart.at[2])

    def both(body, *rows):
        for e in rows:
            body(e, 0)

    c, new_c = c_a, c_b
    last = H + ROWS - 1
    for f in range(FINE):
        def step_full(e, z0):
            advance(c, new_c, f, e, z0, 1, True)

        def faces(e, z0):
            face_block(new_c, e, z0, False)

        def first_p(e, z0):
            first_pressure(new_c, e, z0)

        def sweep_1(e, z0):
            sweep(p1, p_a, e, z0)

        def sweep_2(e, z0):
            sweep(p_a, p_b, e, z0)

        def sweep_3(e, z0):
            sweep(p_b, p_a, e, z0)

        base = 6 + 10 * f
        over((H + 1, last), step_full)
        fraction_mid = row_copies([(new_c, 1, 2)], base)
        start(fraction_mid)
        landed(near)
        both(step_full, H, last)
        fraction_far = row_copies([(new_c, 3, 1)], base + 1)
        start(fraction_far)
        over((H + 1, last), first_p)
        pressure_mid = row_copies([(p1, 1, 2)], base + 2)
        start(pressure_mid)
        if f == 0:
            hear(hand_sem.at[0], [(1, 0), (-1, 0)])
            tell(hand_sem.at[1], [(2, 0), (-2, 0)])
            each_target(starts, cstart.at[2], "start")
        else:
            hear(hand_sem.at[1], [(2, 0), (-2, 0)])
            tell(hand_sem.at[2], [(0, 4), (0, -4)])
        landed(far)
        advance(c, new_c, f, H - 1, 0, 0, False)
        advance(c, new_c, f, last + 1, 0, 2, False)
        both(first_p, H, last)
        pressure_near = row_copies([(p1, 0, 1)], base + 3)
        pressure_far = row_copies([(p1, 3, 1)], base + 4)
        start(pressure_near)
        start(pressure_far)
        over((H + 1, last), sweep_1)
        landed(fraction_mid)
        both(faces, H - 1, last + 1)
        landed(fraction_far)
        both(faces, H - 2, last + 2)
        both(faces, H - 3, last + 3)
        if f == 0:
            each_source(starts, cstart.at[2])
            done = diffuse_down(cstart, 2, 2)
            prev[...] = done[0] * (t > 0).astype(F32)
        else:
            hear(hand_sem.at[2], [(0, 4), (0, -4)])
            tell(hand_sem.at[3], [(-k, 0) for k in (1, 2, 3, 4)])
        landed(pressure_mid)
        landed(pressure_near)
        both(sweep_1, H, last)
        both(sweep_1, H - 1, last + 1)
        both(sweep_1, H - 2, last + 2)
        over((H - 1, last + 2), sweep_2)
        over((H, last + 1), sweep_3)
        landed(pressure_far)
        both(sweep_1, H - 3, last + 3)
        both(sweep_2, H - 2, last + 2)
        both(sweep_3, H - 1, last + 1)
        sent(near)
        sent(far)
        def end(e, z0):
            project(new_c, e, z0)

        both(end, H, last)
        if f == 0:
            near = row_copies([(u.at[0], 0, 1), (u.at[1], 0, 1), (u.at[2], 0, 1)], 26)
            start(near)
        over((H + 1, last), end)
        if f == 0:
            far = row_copies([(u.at[0], 1, 1)], 29)
            start(far)
        for copies in (fraction_mid, fraction_far, pressure_mid, pressure_near, pressure_far):
            sent(copies)
        c, new_c = new_c, c
    each_target(starts, cstart.at[2], "sent")

    stores = []
    for k in range(SUB):
        cols = pl.ds(LANE * k, LANE)
        stores.append(pltpu.make_async_copy(
            c.at[pl.ds(H, ROWS), pl.ds(1, NZ), k, :], ofrac_ref.at[0, :, :, cols], out_sem.at[0, k]))
        stores.append(pltpu.make_async_copy(
            u.at[:, pl.ds(H, ROWS), pl.ds(1, NZ), k, :], ovel_ref.at[0, :, :, :, cols], out_sem.at[1, k]))
    restrict(c, drive)
    drive[...] = drive[...] - prev[...]
    hear(hand_sem.at[3], [(k, 0) for k in (1, 2, 3, 4)])
    each_target(three_back, drive, "start")
    each_target(two_back, drive, "start")
    each_target(one_back, drive, "start")
    for c_ in stores:
        c_.start()
    each_source(three_back, drive)
    three = diffuse_down(rx3, 6, 2)
    each_source(two_back, drive)
    three[pl.ds(0, 9)] = three[pl.ds(0, 9)] + rx2[...]
    diffuse(three, w0, 7, 3)
    diffuse(w0, w1, 5, 2)
    each_source(one_back, drive)
    w1[pl.ds(0, 5)] = w1[pl.ds(0, 5)] + rx1[...]
    diffuse(w1, w0, 3, 1)
    diffuse(w0, w1, 1, 0)
    part[...] = w1[0]
    each_target(sum_four, part, "start")
    each_target(sum_two, part, "start")
    each_source(sum_four, part)
    eight = diffuse_down(rxq, 8, 4)
    each_source(sum_two, part)
    eight[pl.ds(0, 9)] = eight[pl.ds(0, 9)] + rxs[...]
    four = diffuse_down(eight, 4, 4)
    correction = (part[...] + four[0]) - prev[...]

    for field in range(4):
        m = jnp.where(lax.rem(lane, 4) == field, correction, 0.0)
        m = m + roll(m, 1 if field % 2 == 0 else LANE - 1, 2)
        m = m + roll(m, 2 if field < 2 else LANE - 2, 2)
        wide[field] = jnp.broadcast_to(m[:, None], (4, 4, SUB, LANE)).reshape(NZ, SUB, LANE)
    for k in range(SUB):
        cols = pl.ds(LANE * k, LANE)
        stores.append(pltpu.make_async_copy(wide.at[0, :, k, :], cfrac_ref.at[:, cols], out_sem.at[2, k]))
        stores.append(pltpu.make_async_copy(wide.at[1:4, :, k, :], cvel_ref.at[:, :, cols], out_sem.at[3, k]))
        stores[-2].start()
        stores[-1].start(priority=1)
    each_target(three_back, drive, "sent")
    each_target(two_back, drive, "sent")
    each_target(one_back, drive, "sent")
    each_target(sum_four, part, "sent")
    each_target(sum_two, part, "sent")
    for c_ in stores:
        c_.wait()


def add_kernel(frac_ref, vel_ref, frac_off, vel_off, ofrac_ref, ovel_ref):
    ofrac_ref[...] = frac_ref[...] + frac_off[...][None, None]
    ovel_ref[...] = vel_ref[...] + vel_off[...][None, :, None]


def shards(fraction_levels, start_velocity, electrode_plan):
    line = (SUB, LANE)
    pad = (EXT, NZ + 2) + line
    flat = (EXT, NZ) + line
    row = (4,) + line

    def vmem(*shape):
        return pltpu.VMEM(shape, F32)

    end_fraction, end_velocity, fraction_off, velocity_off = pl.pallas_call(
        kernel,
        out_shape=(
            jax.ShapeDtypeStruct(fraction_levels.shape, F32),
            jax.ShapeDtypeStruct(start_velocity.shape, F32),
            jax.ShapeDtypeStruct(fraction_levels.shape[2:], F32),
            jax.ShapeDtypeStruct((3,) + fraction_levels.shape[2:], F32),
        ),
        in_specs=[
            pl.BlockSpec(memory_space=pl.ANY),
            pl.BlockSpec(memory_space=pl.ANY),
            pl.BlockSpec(memory_space=pltpu.SMEM),
        ],
        out_specs=(pl.BlockSpec(memory_space=pl.ANY),) * 4,
        scratch_shapes=[
            pltpu.VMEM((ROWS, NZ) + line, jnp.int32),
            vmem(*pad), vmem(*pad),
            vmem(3, *pad), vmem(3, *pad),
            vmem(EXT + 1, NZ, *line), vmem(*pad), vmem(*flat), vmem(*flat), vmem(*flat),
            vmem(*pad), vmem(*pad), vmem(*pad),
            vmem(FINE, 3, *line), vmem(NZ, *line),
            vmem(5, *row), vmem(*row), vmem(*row),
            vmem(5, *row), vmem(9, *row), vmem(13, *row), vmem(9, *row), vmem(17, *row),
            vmem(*row), vmem(17, *row), vmem(17, *row), vmem(4, NZ, *line),
            pltpu.SemaphoreType.DMA((2, ROWS, SUB)), pltpu.SemaphoreType.DMA((4, SUB)),
            pltpu.SemaphoreType.DMA((30, 2)), pltpu.SemaphoreType.DMA((30, 2)),
            pltpu.SemaphoreType.DMA((58,)), pltpu.SemaphoreType.DMA((58,)),
            pltpu.SemaphoreType.REGULAR((4,)),
        ],
        compiler_params=pltpu.CompilerParams(
            collective_id=0, has_side_effects=True, vmem_limit_bytes=62 * 2**20
        ),
    )(fraction_levels, start_velocity, electrode_plan)
    def frac(i):
        return 0, i, 0, 0

    def vel(i):
        return 0, 0, i, 0, 0

    layers, columns = fraction_levels.shape[2:]
    frac_spec = pl.BlockSpec((1, ROWS, layers, columns), frac)
    vel_spec = pl.BlockSpec((1, 3, ROWS, layers, columns), vel)
    return pl.pallas_call(
        add_kernel,
        grid=(1,),
        out_shape=(
            jax.ShapeDtypeStruct(end_fraction.shape, F32),
            jax.ShapeDtypeStruct(end_velocity.shape, F32),
        ),
        in_specs=[
            frac_spec, vel_spec,
            pl.BlockSpec((layers, columns), lambda i: (0, 0)),
            pl.BlockSpec((3, layers, columns), lambda i: (0, 0, 0)),
        ],
        out_specs=(frac_spec, vel_spec),
    )(end_fraction, end_velocity, fraction_off, velocity_off)


def solution(mesh):
    return jax.shard_map(
        shards,
        mesh=mesh,
        in_specs=(
            P("tm", "space", None, None),
            P("tm", None, "space", None, None),
            P("tm", None, None),
        ),
        out_specs=(P("tm", "space", None, None), P("tm", None, "space", None, None)),
        check_vma=False,
    )
```
